128 devices in a mesh: ctx: 16 (over z, y), hg: 8 (over x, core).
Axes of the slice: x: 4, y: 4, z: 4, core: 2. Of those that a mesh axis runs over, the one named last changes fastest.
Arguments:
- queries: bfloat16 [2, 16, 8192, 256], P(None, None, ('ctx', 'hg')), may hold values from -6 to 6
- keys: bfloat16 [2, 16, 8192, 256], P(None, None, ('ctx', 'hg')), may hold values from -6 to 6
- values: bfloat16 [2, 16, 8192, 256], P(None, None, ('ctx', 'hg')), may hold values from -6 to 6
- rates: bfloat16 [2, 16, 8192], P(None, None, ('ctx', 'hg')), may hold values from 0.099609375 to 1
- step_sizes: float32 [16], P('hg'), may hold values from 0.3 to 1.5
- w_gate: float32 [16, 256, 1024], P('hg'), may hold values from -0.375 to 0.375
- w_up: float32 [16, 256, 1024], P('hg'), may hold values from -0.375 to 0.375
- w_down: float32 [16, 256, 1024], P('hg'), may hold values from -0.1875 to 0.1875
Outputs:
- outputs: float32 [2, 16, 8192, 256], P(None, None, ('ctx', 'hg'))
- gate_final: float32 [16, 256, 1024], P('hg')
- up_final: float32 [16, 256, 1024], P('hg')
- down_final: float32 [16, 256, 1024], P('hg')
The draws below stay inside these ranges and needn't reach their ends.
All inputs are finite; a program needn't handle non-finite values.
Results may differ from the reference program's by a relative error of at most 0.039.
Values may be sent and summed in bfloat16 or wider, within the bound.
No kernel may reach another device: no remote copies, remote signals or barrier semaphores. Data moves between devices by JAX's collectives and lax.ppermute only.
A program may use at most 128 MiB of HBM per device.

```python
import math
import jax
import jax.numpy as jnp
from jax import lax

DH = 256
FF = 1024
HEADS = 16
GROUPS = 2
NS_STEPS = 5
TOKENS = 8192


def levels(own_key, extent, shards, low, top_value):
    def one(position, shards_of):
        steps = jax.random.uniform(jax.random.fold_in(jax.random.fold_in(own_key, 6), position), (shards_of,), jnp.float32, low / len(shards), top_value / len(shards))
        return jnp.repeat(jnp.exp(steps), extent[position] // shards_of).reshape((-1,) + (1,) * (len(extent) - position - 1))

    loudness = one(*shards[0])
    for cut in shards[1:]:
        loudness = loudness * one(*cut)
    return loudness


def bell_draw(own_key, extent, scale, reach, pieces=(), held_as=jnp.bfloat16):
    entries = jax.random.normal(own_key, extent, jnp.float32) * scale
    if len(pieces) > 0:
        entries = levels(own_key, extent, pieces, -0.22, 0.18) * entries
    return jnp.clip(entries, min=-reach, max=reach).astype(held_as)


def setup_inputs(seed: int = 0) -> dict:
    streams_of = jax.random.split(jax.random.key(seed), 9)
    return {
        "queries": bell_draw(streams_of[0], (GROUPS, HEADS, TOKENS, DH), 1.0, 6.0, ((2, 128),)),
        "keys": bell_draw(streams_of[1], (GROUPS, HEADS, TOKENS, DH), 1.0, 6.0, ((2, 128),)),
        "values": bell_draw(streams_of[2], (GROUPS, HEADS, TOKENS, DH), 1.0, 6.0, ((2, 128),)),
        "rates": jnp.clip(jnp.exp(math.log(1.0) - 2.306499 * jax.random.uniform(streams_of[3], (GROUPS, HEADS, TOKENS), jnp.float32) ** levels(streams_of[3], (GROUPS, HEADS, TOKENS), ((2, 128),), -0.2, 0.2)), 0.099609375, 1.0).astype(jnp.bfloat16),
        "step_sizes": jnp.clip(jnp.exp(math.log(1.5) - 1.60943787 * jax.random.uniform(streams_of[4], (HEADS,), jnp.float32) ** levels(streams_of[4], (HEADS,), ((0, 8),), -0.2, 0.2)), 0.3, 1.5),
        "w_gate": bell_draw(streams_of[5], (HEADS, DH, FF), DH ** -0.5, 0.375, ((0, 8),), jnp.float32),
        "w_up": bell_draw(streams_of[6], (HEADS, DH, FF), DH ** -0.5, 0.375, ((0, 8),), jnp.float32),
        "w_down": bell_draw(streams_of[7], (HEADS, DH, FF), FF ** -0.5, 0.1875, ((0, 8),), jnp.float32),
    }


coef_a = 3.4445
coef_b = -4.775
coef_c = 2.0315

def newton_schulz(grad):
    rounded = grad.astype(jnp.bfloat16).astype(jnp.float32)
    total = jnp.sum(rounded * rounded)
    ortho = (rounded / (jnp.sqrt(total) + 1e-07)).astype(jnp.bfloat16)
    for step in range(NS_STEPS):
        gram = jnp.dot(ortho, ortho.T, preferred_element_type=jnp.float32).astype(jnp.bfloat16)
        square = jnp.dot(gram, gram, preferred_element_type=jnp.float32)
        poly = (coef_b * gram.astype(jnp.float32) + coef_c * square).astype(jnp.bfloat16)
        ortho = (coef_a * ortho.astype(jnp.float32) + jnp.dot(poly, ortho, preferred_element_type=jnp.float32)).astype(jnp.bfloat16)
    return ortho

def renew(weight, grad, step):
    cand = weight - step * newton_schulz(grad).astype(jnp.float32)
    scale = jnp.sqrt(lax.optimization_barrier(jnp.sum(weight * weight, axis=0, keepdims=True)) + 1e-06) / jnp.sqrt(lax.optimization_barrier(jnp.sum(cand * cand, axis=0, keepdims=True)) + 1e-06)
    return cand * scale

def one_head(items):
    query_h, key_h, value_h, rate_h, step, gate_w, up_w, down_w = items
    outs = []
    for group in range(GROUPS):
        gate_b = gate_w.astype(jnp.bfloat16)
        up_b = up_w.astype(jnp.bfloat16)
        down_b = down_w.astype(jnp.bfloat16)
        key_c = key_h[group]
        gate = jnp.dot(key_c, gate_b, preferred_element_type=jnp.float32)
        upval = jnp.dot(key_c, up_b, preferred_element_type=jnp.float32)
        active = jax.nn.silu(gate)
        hidden = (active * upval).astype(jnp.bfloat16)
        dout = (-rate_h[group].astype(jnp.float32)[:, None] * value_h[group].astype(jnp.float32)).astype(jnp.bfloat16)
        grad_down = jnp.dot(dout.T, hidden, preferred_element_type=jnp.float32)
        dhid = jnp.dot(dout, down_b, preferred_element_type=jnp.float32)
        sigma = jax.nn.sigmoid(gate)
        d_gate = (dhid * upval * sigma * (1.0 + gate * (1.0 - sigma))).astype(jnp.bfloat16)
        d_up = (dhid * active).astype(jnp.bfloat16)
        grad_gate = jnp.dot(key_c.T, d_gate, preferred_element_type=jnp.float32)
        grad_up = jnp.dot(key_c.T, d_up, preferred_element_type=jnp.float32)
        gate_w = renew(gate_w, grad_gate, step)
        up_w = renew(up_w, grad_up, step)
        down_w = renew(down_w, grad_down, step)
        query_c = query_h[group]
        q_gate = jnp.dot(query_c, gate_w.astype(jnp.bfloat16), preferred_element_type=jnp.float32)
        q_up = jnp.dot(query_c, up_w.astype(jnp.bfloat16), preferred_element_type=jnp.float32)
        q_hid = (jax.nn.silu(q_gate) * q_up).astype(jnp.bfloat16)
        result = jnp.dot(q_hid, down_w.astype(jnp.bfloat16).T, preferred_element_type=jnp.float32)
        outs.append(result)
    return (jnp.stack(outs), gate_w, up_w, down_w)

def reference(queries, keys, values, rates, step_sizes, w_gate, w_up, w_down):
    items = (jnp.moveaxis(queries, 1, 0), jnp.moveaxis(keys, 1, 0), jnp.moveaxis(values, 1, 0), jnp.moveaxis(rates, 1, 0), step_sizes, w_gate, w_up, w_down)
    outs, gate_final, up_final, down_final = lax.map(one_head, items)
    return (jnp.moveaxis(outs, 0, 1), gate_final, up_final, down_final)
```

```python
import functools

import jax
import jax.numpy as jnp
from jax import lax
from jax.experimental import pallas as pl
from jax.experimental.pallas import tpu as pltpu
from jax.sharding import Mesh
from jax.sharding import PartitionSpec as P

GROUPS = 2
NS_STEPS = 5
DH = 256
FF = 1024
HALF = FF // 2
LANE = 128
TOK = 1024
TILE = 512

coef_a = 3.4445
coef_b = -4.775
coef_c = 2.0315

VMEM_LIMIT = 48 * 1024 * 1024
f32 = jnp.float32
bf16 = jnp.bfloat16


def dot(a, b, dims):
    return lax.dot_general(a, b, (dims, ((), ())), preferred_element_type=f32)


def params():
    return pltpu.CompilerParams(vmem_limit_bytes=VMEM_LIMIT)


VSPEC = pl.BlockSpec(memory_space=pltpu.VMEM)
SSPEC = pl.BlockSpec(memory_space=pltpu.SMEM)


def grad_kernel(own_ref, peer_ref, wb_ref, out_ref, acc_ref):
    first = True
    for kd_ref in (own_ref, peer_ref):
        for tile in range(TOK // TILE):
            rows = pl.ds(tile * TILE, TILE)
            key = kd_ref[rows, :DH]
            dout = kd_ref[rows, DH : 2 * DH]
            gate = dot(key, wb_ref[0], ((1,), (0,)))
            up = dot(key, wb_ref[1], ((1,), (0,)))
            dhid = dot(dout, wb_ref[2], ((1,), (0,)))
            sigma = jax.nn.sigmoid(gate)
            active = gate * sigma
            hidden = (active * up).astype(bf16)
            d_up = (dhid * active).astype(bf16)
            d_gate = (dhid * up * sigma * (1.0 + gate * (1.0 - sigma))).astype(bf16)
            for index, (left, right) in enumerate(((key, d_gate), (key, d_up), (dout, hidden))):
                part = dot(left, right, ((0,), (0,)))
                if first:
                    acc_ref[index] = part
                else:
                    acc_ref[index] += part
            first = False
    for chunk in range(4):
        for index in range(3):
            out_ref[chunk, index] = acc_ref[index, :, chunk * LANE : (chunk + 1) * LANE].astype(bf16)


def grads(own, peer, wb):
    spec = pl.BlockSpec((TOK, 2 * DH), lambda i: (0, 0))
    return pl.pallas_call(
        grad_kernel,
        grid=(1,),
        out_shape=jax.ShapeDtypeStruct((4, 3, DH, LANE), bf16),
        in_specs=[spec, spec, pl.BlockSpec((3, DH, HALF), lambda i: (0, 0, 0))],
        out_specs=pl.BlockSpec((4, 3, DH, LANE), lambda i: (0, 0, 0, 0)),
        scratch_shapes=[pltpu.VMEM((3, DH, HALF), f32)],
        compiler_params=params(),
        name="grads",
        cost_estimate=pl.CostEstimate(
            flops=6 * 2 * 2 * TOK * DH * HALF, bytes_accessed=4 << 20, transcendentals=2 * TOK * HALF
        ),
    )(own, peer, wb)


def ns_kernel(*refs):
    g_refs = refs[:8]
    w_ref, step_ref, x_ref, wnew_ref, wb_ref, ortho = refs[8:]
    for index in range(3):
        total = jnp.zeros((), f32)
        for g_ref in g_refs:
            part = g_ref[index].astype(f32)
            total = total + jnp.sum(part * part)
        norm = jnp.sqrt(jnp.full((1, 1), total, f32)) + 1e-07
        for chunk, g_ref in enumerate(g_refs):
            ortho[index, :, chunk * LANE : (chunk + 1) * LANE] = (g_ref[index].astype(f32) / norm).astype(bf16)
    for _ in range(NS_STEPS):
        grams = [dot(ortho[i], ortho[i], ((1,), (1,))).astype(bf16) for i in range(3)]
        squares = [dot(gram, gram, ((1,), (0,))) for gram in grams]
        polys = [
            (coef_b * gram.astype(f32) + coef_c * square).astype(bf16) for gram, square in zip(grams, squares)
        ]
        for i in range(3):
            moved = dot(polys[i], ortho[i], ((1,), (0,)))
            ortho[i] = (coef_a * ortho[i].astype(f32) + moved).astype(bf16)
    step = step_ref[0]
    for index in range(3):
        for chunk in range(8):
            cols = slice(chunk * LANE, (chunk + 1) * LANE)
            value = ortho[index, :, cols]
            x_ref[chunk, index] = value
            weight = w_ref[chunk, index]
            fresh = renew(weight, value, step)
            wnew_ref[chunk, index] = fresh
            wb_ref[index, :, cols] = fresh.astype(bf16)


def renew(weight, value, step):
    cand = weight - step * value.astype(f32)
    scale = jnp.sqrt(jnp.sum(weight * weight, axis=0, keepdims=True) + 1e-06) / jnp.sqrt(
        jnp.sum(cand * cand, axis=0, keepdims=True) + 1e-06
    )
    return cand * scale


def newton(chunks, weight, step):
    return pl.pallas_call(
        ns_kernel,
        out_shape=(
            jax.ShapeDtypeStruct((8, 3, DH, LANE), bf16),
            jax.ShapeDtypeStruct((8, 3, DH, LANE), f32),
            jax.ShapeDtypeStruct((3, DH, FF), bf16),
        ),
        in_specs=[VSPEC] * 9 + [SSPEC],
        out_specs=(VSPEC, VSPEC, VSPEC),
        scratch_shapes=[pltpu.VMEM((3, DH, FF), bf16)],
        compiler_params=params(),
        name="newton",
        cost_estimate=pl.CostEstimate(flops=3 * 1510 * 10**6, bytes_accessed=11 << 20, transcendentals=0),
    )(*chunks, weight, step)


def query_kernel(q_ref, wb_ref, out_ref):
    for tile in range(TOK // TILE):
        rows = pl.ds(tile * TILE, TILE)
        query = q_ref[rows, :]
        gate = dot(query, wb_ref[0], ((1,), (0,)))
        up = dot(query, wb_ref[1], ((1,), (0,)))
        hidden = (gate * jax.nn.sigmoid(gate) * up).astype(bf16)
        out_ref[rows, :] = dot(hidden, wb_ref[2], ((1,), (1,))).astype(bf16)


def forward(rest, wb, column):
    return pl.pallas_call(
        query_kernel,
        grid=(1,),
        out_shape=jax.ShapeDtypeStruct((TOK, DH), bf16),
        in_specs=[
            pl.BlockSpec((TOK, DH), lambda i: (0, column)),
            pl.BlockSpec((3, DH, FF), lambda i: (0, 0, 0)),
        ],
        out_specs=pl.BlockSpec((TOK, DH), lambda i: (0, 0)),
        compiler_params=params(),
        name="forward",
        cost_estimate=pl.CostEstimate(
            flops=3 * 2 * TOK * DH * FF, bytes_accessed=3 << 20, transcendentals=TOK * FF
        ),
    )(rest, wb)


def prep_kernel(place_ref, local_ref, other_ref, wrot_ref, wb_ref):
    core, deep, mine = place_ref[0], place_ref[1], place_ref[2]
    for half in range(2):
        for chunk in range(4):
            block = (core ^ half) * 4 + ((deep + chunk) & 3)
            cols = pl.ds(pl.multiple_of(block * LANE, LANE), LANE)
            for index in range(3):
                weight = jnp.where(mine == 1, local_ref[index, :, cols], other_ref[index, :, cols])
                wrot_ref[half * 4 + chunk, index] = weight
                at = (half * 4 + chunk) * LANE
                wb_ref[index, :, at : at + LANE] = weight.astype(bf16)


def prepare(place, local, other):
    return pl.pallas_call(
        prep_kernel,
        out_shape=(
            jax.ShapeDtypeStruct((8, 3, DH, LANE), f32),
            jax.ShapeDtypeStruct((3, DH, FF), bf16),
        ),
        in_specs=[SSPEC, VSPEC, VSPEC],
        out_specs=(VSPEC, VSPEC),
        compiler_params=params(),
        name="prepare",
        cost_estimate=pl.CostEstimate(flops=10**6, bytes_accessed=11 << 20, transcendentals=0),
    )(place, local, other)


def final_kernel(place_ref, step_ref, *refs):
    firsts, seconds, weights, outs = refs[:4], refs[4:8], refs[8:11], refs[11:14]
    core, deep, row = place_ref[0], place_ref[1], place_ref[2]
    head = pl.program_id(0)
    step = step_ref[head]
    away = (row - 2 * core - head) & 3

    def run(first_ref, second_ref):
        for chunk in range(4):
            at = (chunk - deep) & 3
            cols = slice(chunk * LANE, (chunk + 1) * LANE)
            for index in range(3):
                weight = weights[index][0, :, cols]
                weight = renew(weight, first_ref[at, index], step)
                outs[index][0, :, cols] = renew(weight, second_ref[at, index], step)

    for far in range(4):
        pl.when(away == far)(functools.partial(run, firsts[far], seconds[far]))


def finish(place, steps, firsts, seconds, weights):
    def x_map(far):
        def index(head, half, place_ref, step_ref):
            away = (place_ref[2] - 2 * place_ref[0] - head) & 3
            return (jnp.where(away == far, place_ref[0] ^ half, 0), 0, 0, 0)

        return index

    wspec = pl.BlockSpec((1, DH, HALF), lambda head, half, p, s: (head, 0, half))
    xspecs = [pl.BlockSpec((4, 3, DH, LANE), x_map(far)) for far in range(4)]
    return pl.pallas_call(
        final_kernel,
        grid_spec=pltpu.PrefetchScalarGridSpec(
            num_scalar_prefetch=2,
            grid=(2, 2),
            in_specs=xspecs + xspecs + [wspec] * 3,
            out_specs=[wspec] * 3,
        ),
        out_shape=[jax.ShapeDtypeStruct((2, DH, FF), f32)] * 3,
        compiler_params=params(),
        name="finish",
        cost_estimate=pl.CostEstimate(flops=2 * 10**7, bytes_accessed=16 << 20, transcendentals=0),
    )(place, steps, *firsts, *seconds, *weights)


def turn(far):
    return [(i, (i + far) % 4) for i in range(4)]


SWAP = [(0, 1), (1, 0)]


def swap(value):
    return lax.ppermute(value, "c", SWAP)


def sum_all(partial):
    received = [lax.ppermute(partial[far], "z", turn(far)) for far in (1, 2, 3)]
    total = partial[0].astype(f32)
    for part in received:
        total = total + part.astype(f32)
    mine = total.astype(bf16)
    chunks = [mine] + [lax.ppermute(mine, "z", turn(4 - far)) for far in (1, 2, 3)]
    return chunks + [swap(chunk) for chunk in chunks]


def spread(value):
    got = [value]
    for far in (1, 2, 3):
        pairs = [(2 * y + y // 2, 2 * ((y + far) % 4) + y // 2) for y in range(4)]
        got.append(lax.ppermute(value, ("y", "c"), pairs))
    return got


def shards(queries, keys, values, rates, step_sizes, w_gate, w_up, w_down):
    z, y, c = lax.axis_index("z"), lax.axis_index("y"), lax.axis_index("c")
    dout = (-rates.astype(f32)[..., None] * values.astype(f32)).astype(bf16)
    exchange = functools.partial(
        lax.all_to_all, axis_name=("x", "y"), split_axis=0, concat_axis=0, tiled=True
    )
    first = exchange(jnp.concatenate([keys[0], dout[0]], axis=-1)).reshape(TOK, 2 * DH)
    rest = exchange(
        jnp.concatenate([keys[1], dout[1], queries[0], queries[1]], axis=-1)
    ).reshape(TOK, 4 * DH)
    mine = (c == y // 2).astype(jnp.int32)
    pick = lambda w: lax.dynamic_index_in_dim(w, y % 2, 0, keepdims=False)
    local = jnp.stack([pick(w_gate), pick(w_up), pick(w_down)])
    step_local = jnp.broadcast_to(pick(step_sizes), (8, 128))
    step = jnp.where(mine == 1, step_local, swap(step_local))[0, :1]
    place = jnp.stack([c, z, mine]).astype(jnp.int32)
    weights, wb = prepare(place, local, swap(local))
    outs, spreads = [], []
    for group in range(GROUPS):
        own = first if group == 0 else rest
        peer = swap(own if group == 0 else own[:, : 2 * DH])
        partial = grads(own, peer, wb)
        ortho, weights, wb = newton(sum_all(partial), weights, step)
        spreads.append(spread(ortho))
        result = forward(rest, wb, 2 + group)
        outs.append(exchange(result.reshape(16, 64, DH)))
    place = jnp.stack([c, z, y]).astype(jnp.int32)
    gate, up, down = finish(place, step_sizes, spreads[0], spreads[1], (w_gate, w_up, w_down))
    return (jnp.stack(outs).astype(f32), gate, up, down)


def solution(mesh):
    grid = Mesh(mesh.devices.reshape(4, 4, 4, 2), ("z", "y", "x", "c"))
    tokens = ("z", "y", "x", "c")
    heads = ("x", "c")
    return jax.shard_map(
        shards,
        mesh=grid,
        in_specs=(
            P(None, None, tokens, None),
            P(None, None, tokens, None),
            P(None, None, tokens, None),
            P(None, None, tokens),
            P(heads),
            P(heads, None, None),
            P(heads, None, None),
            P(heads, None, None),
        ),
        out_specs=(
            P(None, None, tokens, None),
            P(heads, None, None),
            P(heads, None, None),
            P(heads, None, None),
        ),
        check_vma=False,
    )
```

```python
import functools

import jax
import jax.numpy as jnp
from jax import lax
from jax.experimental import pallas as pl
from jax.experimental.pallas import tpu as pltpu
from jax.sharding import Mesh
from jax.sharding import PartitionSpec as P

GROUPS = 2
NS_STEPS = 5
DH = 256
FF = 1024
HALF = FF // 2
LANE = 128
TOK = 1024
TILE = 512

coef_a = 3.4445
coef_b = -4.775
coef_c = 2.0315

f32 = jnp.float32
bf16 = jnp.bfloat16
MIB = 1024 * 1024

VSPEC = pl.BlockSpec(memory_space=pltpu.VMEM)
SSPEC = pl.BlockSpec(memory_space=pltpu.SMEM)


def dot(a, b, dims):
    return lax.dot_general(a, b, (dims, ((), ())), preferred_element_type=f32)


def params(mib):
    return pltpu.CompilerParams(vmem_limit_bytes=mib * MIB)


def cost(flops, size, transcendentals=0):
    return pl.CostEstimate(flops=flops, bytes_accessed=size, transcendentals=transcendentals)


def after(value, *earlier):
    return lax.optimization_barrier((value, earlier))[0]


def pack_kernel(key_ref, value_ref, rate_ref, *refs):
    out_ref = refs[-1]
    out_ref[:, :, :DH] = key_ref[0]
    rate = -rate_ref[0].astype(f32)
    out_ref[:, :, DH : 2 * DH] = (rate[:, :, None] * value_ref[0].astype(f32)).astype(bf16)
    if len(refs) > 1:
        for group in range(GROUPS):
            out_ref[:, :, (2 + group) * DH : (3 + group) * DH] = refs[0][group]


def pack(group, keys, values, rates, *queries):
    spec = pl.BlockSpec((1, 16, 64, DH), lambda i: (group, 0, 0, 0))
    width = (2 + 2 * len(queries)) * DH
    return pl.pallas_call(
        pack_kernel,
        grid=(1,),
        out_shape=jax.ShapeDtypeStruct((16, 64, width), bf16),
        in_specs=[spec, spec, pl.BlockSpec((1, 16, 64), lambda i: (group, 0, 0))]
        + [pl.BlockSpec((2, 16, 64, DH), lambda i: (0, 0, 0, 0))] * len(queries),
        out_specs=pl.BlockSpec((16, 64, width), lambda i: (0, 0, 0)),
        compiler_params=params(16),
        name="pack",
        cost_estimate=cost(10**6, 4 * 1024 * width),
    )(keys, values, rates, *queries)


def grad_kernel(own_ref, peer_ref, wb_ref, *refs):
    out_refs, acc_ref = refs[:4], refs[4]
    first = True
    for kd_ref in (own_ref, peer_ref):
        for tile in range(TOK // TILE):
            rows = pl.ds(tile * TILE, TILE)
            key = kd_ref[rows, :DH]
            dout = kd_ref[rows, DH : 2 * DH]
            gate = dot(key, wb_ref[0], ((1,), (0,)))
            up = dot(key, wb_ref[1], ((1,), (0,)))
            dhid = dot(dout, wb_ref[2], ((1,), (0,)))
            sigma = jax.nn.sigmoid(gate)
            active = gate * sigma
            hidden = (active * up).astype(bf16)
            d_up = (dhid * active).astype(bf16)
            d_gate = (dhid * up * sigma * (1.0 + gate * (1.0 - sigma))).astype(bf16)
            for index, (left, right) in enumerate(((key, d_gate), (key, d_up), (dout, hidden))):
                part = dot(left, right, ((0,), (0,)))
                if first:
                    acc_ref[index] = part
                else:
                    acc_ref[index] += part
            first = False
    for chunk in range(4):
        for index in range(3):
            out_refs[chunk][index] = acc_ref[index, :, chunk * LANE : (chunk + 1) * LANE].astype(bf16)


def grads(own, peer, wb):
    spec = pl.BlockSpec((TOK, 2 * DH), lambda i: (0, 0))
    piece = jax.ShapeDtypeStruct((3, DH, LANE), bf16)
    return pl.pallas_call(
        grad_kernel,
        grid=(1,),
        out_shape=[piece] * 4,
        in_specs=[spec, spec, pl.BlockSpec((3, DH, HALF), lambda i: (0, 0, 0))],
        out_specs=[pl.BlockSpec((3, DH, LANE), lambda i: (0, 0, 0))] * 4,
        scratch_shapes=[pltpu.VMEM((3, DH, HALF), f32)],
        compiler_params=params(24),
        name="grads",
        cost_estimate=cost(12 * 2 * TOK * DH * HALF, 4 * MIB, 2 * TOK * HALF),
    )(own, peer, wb)


def ns_kernel(*refs):
    g_refs, w_ref, step_ref = refs[:8], refs[8], refs[9]
    halves, more, ortho = refs[10:12], refs[12:-1], refs[-1]
    for index in range(3):
        total = None
        for g_ref in g_refs:
            part = g_ref[index].astype(f32)
            part = part * part
            total = part if total is None else total + part
        total = jnp.sum(jnp.sum(total, axis=0, keepdims=True), axis=1, keepdims=True)
        norm = jnp.sqrt(total) + 1e-07
        for chunk, g_ref in enumerate(g_refs):
            ortho[index, :, chunk * LANE : (chunk + 1) * LANE] = (g_ref[index].astype(f32) / norm).astype(bf16)
    for _ in range(NS_STEPS):
        grams = [dot(ortho[i], ortho[i], ((1,), (1,))).astype(bf16) for i in range(3)]
        squares = [dot(gram, gram, ((1,), (0,))) for gram in grams]
        polys = [
            (coef_b * gram.astype(f32) + coef_c * square).astype(bf16) for gram, square in zip(grams, squares)
        ]
        for i in range(3):
            moved = dot(polys[i], ortho[i], ((1,), (0,)))
            ortho[i] = (coef_a * ortho[i].astype(f32) + moved).astype(bf16)
    step = step_ref[0:1, 0:1]
    for index in range(3):
        for chunk in range(8):
            value = ortho[index, :, chunk * LANE : (chunk + 1) * LANE]
            fresh = renew(w_ref[chunk, index], value, step)
            at = (chunk % 4) * LANE
            halves[chunk // 4][index, :, at : at + LANE] = fresh.astype(bf16)
            if more:
                more[0][chunk, index] = fresh


def renew(weight, value, step):
    cand = weight - step * value.astype(f32)
    scale = jnp.sqrt(jnp.sum(weight * weight, axis=0, keepdims=True) + 1e-06) / jnp.sqrt(
        jnp.sum(cand * cand, axis=0, keepdims=True) + 1e-06
    )
    return cand * scale


def newton(chunks, weight, step, last):
    half = jax.ShapeDtypeStruct((3, DH, HALF), bf16)
    outs = [half, half]
    if not last:
        outs.append(jax.ShapeDtypeStruct((8, 3, DH, LANE), f32))
    return pl.pallas_call(
        ns_kernel,
        out_shape=outs,
        in_specs=[VSPEC] * 10,
        out_specs=[VSPEC] * len(outs),
        scratch_shapes=[pltpu.VMEM((3, DH, FF), bf16)],
        compiler_params=params(24),
        name="newton",
        cost_estimate=cost(3 * 1510 * 10**6, 6 * MIB),
    )(*chunks, weight, step)


def query_kernel(q_ref, *refs):
    halves, out_ref = refs[:2], refs[2]
    for tile in range(TOK // TILE):
        rows = pl.ds(tile * TILE, TILE)
        query = q_ref[rows, :]
        total = None
        for wb_ref in halves:
            gate = dot(query, wb_ref[0], ((1,), (0,)))
            up = dot(query, wb_ref[1], ((1,), (0,)))
            hidden = (gate * jax.nn.sigmoid(gate) * up).astype(bf16)
            part = dot(hidden, wb_ref[2], ((1,), (1,)))
            total = part if total is None else total + part
        out_ref[rows, :] = total.astype(bf16)


def forward(rest, wbs, column):
    wspec = pl.BlockSpec((3, DH, HALF), lambda i: (0, 0, 0))
    return pl.pallas_call(
        query_kernel,
        grid=(1,),
        out_shape=jax.ShapeDtypeStruct((TOK, DH), bf16),
        in_specs=[pl.BlockSpec((TOK, DH), lambda i: (0, column)), wspec, wspec],
        out_specs=pl.BlockSpec((TOK, DH), lambda i: (0, 0)),
        compiler_params=params(24),
        name="forward",
        cost_estimate=cost(6 * TOK * DH * FF, 3 * MIB, TOK * FF),
    )(rest, *wbs)


def pick_kernel(row_ref, *refs):
    for index in range(3):
        refs[3][index] = refs[index][0]


def pick(row, weights):
    spec = pl.BlockSpec((1, DH, FF), lambda i, row_ref: (row_ref[0], 0, 0))
    return pl.pallas_call(
        pick_kernel,
        grid_spec=pltpu.PrefetchScalarGridSpec(
            num_scalar_prefetch=1,
            grid=(1,),
            in_specs=[spec] * 3,
            out_specs=pl.BlockSpec((3, DH, FF), lambda i, row_ref: (0, 0, 0)),
        ),
        out_shape=jax.ShapeDtypeStruct((3, DH, FF), f32),
        compiler_params=params(24),
        name="pick",
        cost_estimate=cost(10**5, 6 * MIB),
    )(row, *weights)


def prep_kernel(place_ref, local_ref, other_ref, step_ref, step_other_ref, wrot_ref, one_ref, two_ref, out_ref):
    core, deep, mine = place_ref[0], place_ref[1], place_ref[2]
    out_ref[...] = jnp.where(mine == 1, step_ref[...], step_other_ref[...])
    for half, wb_ref in enumerate((one_ref, two_ref)):
        for chunk in range(4):
            block = (core ^ half) * 4 + ((deep + chunk) & 3)
            cols = pl.ds(pl.multiple_of(block * LANE, LANE), LANE)
            for index in range(3):
                weight = jnp.where(mine == 1, local_ref[index, :, cols], other_ref[index, :, cols])
                wrot_ref[half * 4 + chunk, index] = weight
                wb_ref[index, :, chunk * LANE : (chunk + 1) * LANE] = weight.astype(bf16)


def prepare(place, local, other, step, step_other):
    half = jax.ShapeDtypeStruct((3, DH, HALF), bf16)
    return pl.pallas_call(
        prep_kernel,
        out_shape=(
            jax.ShapeDtypeStruct((8, 3, DH, LANE), f32),
            half,
            half,
            jax.ShapeDtypeStruct((8, LANE), f32),
        ),
        in_specs=[SSPEC] + [VSPEC] * 4,
        out_specs=(VSPEC,) * 4,
        compiler_params=params(24),
        name="prepare",
        cost_estimate=cost(10**6, 11 * MIB),
    )(place, local, other, step, step_other)


def final_kernel(place_ref, *refs):
    got, outs = refs[:8], refs[8:]
    core, deep, row = place_ref[0], place_ref[1], place_ref[2]
    away = (row - 2 * core - pl.program_id(0)) & 3
    flip = core ^ pl.program_id(1)

    def run(ref):
        for chunk in range(4):
            at = pl.multiple_of(((chunk - deep) & 3) * LANE, LANE)
            for index in range(3):
                outs[index][0, :, chunk * LANE : (chunk + 1) * LANE] = ref[index, :, pl.ds(at, LANE)].astype(f32)

    for far in range(4):
        for half in range(2):
            pl.when((away == far) & (flip == half))(functools.partial(run, got[2 * far + half]))


def finish(place, got):
    wspec = pl.BlockSpec((1, DH, HALF), lambda head, half, p: (head, 0, half))
    xspec = pl.BlockSpec((3, DH, HALF), lambda head, half, p: (0, 0, 0))
    return pl.pallas_call(
        final_kernel,
        grid_spec=pltpu.PrefetchScalarGridSpec(
            num_scalar_prefetch=1,
            grid=(2, 2),
            in_specs=[xspec] * 8,
            out_specs=[wspec] * 3,
        ),
        out_shape=[jax.ShapeDtypeStruct((2, DH, FF), f32)] * 3,
        compiler_params=params(32),
        name="finish",
        cost_estimate=cost(10**6, 12 * MIB),
    )(place, *got)


def turn(far):
    return [(i, (i + far) % 4) for i in range(4)]


SWAP = [(0, 1), (1, 0)]


def swap(value):
    return lax.ppermute(value, "c", SWAP)


def gather_sum(partial):
    received = [lax.ppermute(partial[far], "z", turn(far)) for far in (2, 1, 3)]
    total = partial[0].astype(f32)
    for part in received:
        total = total + part.astype(f32)
    mine = total.astype(bf16)
    far2, far1, far3 = [lax.ppermute(mine, "z", turn(4 - far)) for far in (2, 1, 3)]
    chunks = [mine, far1, far2, far3]
    return chunks + [swap(chunk) for chunk in chunks]


def y_pairs(start, end):
    return [(2 * ((y + start) % 4) + y // 2, 2 * ((y + end) % 4) + y // 2) for y in range(4)]


def spread(halves):
    up = [lax.ppermute(half, ("y", "c"), y_pairs(0, 1)) for half in halves]
    down = [lax.ppermute(half, ("y", "c"), y_pairs(0, 3)) for half in halves[::-1]][::-1]
    far = [lax.ppermute(up[0], ("y", "c"), y_pairs(1, 2)), lax.ppermute(down[1], ("y", "c"), y_pairs(3, 2))]
    return list(halves) + up + far + down


def shards(queries, keys, values, rates, step_sizes, w_gate, w_up, w_down):
    z, y, c = lax.axis_index("z"), lax.axis_index("y"), lax.axis_index("c")
    exchange = functools.partial(
        lax.all_to_all, axis_name=("x", "y"), split_axis=0, concat_axis=0, tiled=True
    )
    packed = pack(0, keys, values, rates)
    keys, values, rates, queries, w_gate, w_up, w_down, step_sizes = after(
        (keys, values, rates, queries, w_gate, w_up, w_down, step_sizes), packed
    )
    first = exchange(packed).reshape(TOK, 2 * DH)
    mine = (c == y // 2).astype(jnp.int32)
    local = pick((y % 2)[None].astype(jnp.int32), (w_gate, w_up, w_down))
    step_local = jnp.broadcast_to(lax.dynamic_index_in_dim(step_sizes, y % 2, 0), (8, LANE))
    place = jnp.stack([c, z, mine]).astype(jnp.int32)
    weights, one, two, step = prepare(place, local, swap(local), step_local, swap(step_local))
    wbs = (one, two)
    second = pack(1, keys, values, rates, queries)
    first = after(first, one, second)
    rest = exchange(after(second, first)).reshape(TOK, 4 * DH)

    partial = grads(first, swap(first), wbs[0])
    chunks = gather_sum(partial)
    peer = swap(after(rest, chunks[1:4])[:, : 2 * DH])
    one, two, weights = newton(chunks, weights, step, False)
    wbs = (one, two)

    partial = grads(rest, peer, wbs[0])
    early = exchange(forward(after(rest, partial), wbs, 2).reshape(16, 64, DH))
    chunks = gather_sum(partial)
    wbs = newton(chunks, weights, step, True)
    got = spread(wbs)
    late = exchange(forward(rest, wbs, 3).reshape(16, 64, DH))
    place = jnp.stack([c, z, y]).astype(jnp.int32)
    gate, up, down = finish(place, got)
    return (jnp.stack([early, late]).astype(f32), gate, up, down)


def solution(mesh):
    grid = Mesh(mesh.devices.reshape(4, 4, 4, 2), ("z", "y", "x", "c"))
    tokens = ("z", "y", "x", "c")
    heads = ("x", "c")
    return jax.shard_map(
        shards,
        mesh=grid,
        in_specs=(
            P(None, None, tokens, None),
            P(None, None, tokens, None),
            P(None, None, tokens, None),
            P(None, None, tokens),
            P(heads),
            P(heads, None, None),
            P(heads, None, None),
            P(heads, None, None),
        ),
        out_specs=(
            P(None, None, tokens, None),
            P(heads, None, None),
            P(heads, None, None),
            P(heads, None, None),
        ),
        check_vma=False,
    )
```

```python
import functools

import jax
import jax.numpy as jnp
from jax import lax
from jax.experimental import pallas as pl
from jax.experimental.pallas import tpu as pltpu
from jax.sharding import Mesh
from jax.sharding import PartitionSpec as P

GROUPS = 2
NS_STEPS = 5
DH = 256
FF = 1024
HALF = FF // 2
LANE = 128
TOK = 1024
TILE = 512

coef_a = 3.4445
coef_b = -4.775
coef_c = 2.0315

f32 = jnp.float32
bf16 = jnp.bfloat16
MIB = 1024 * 1024

VSPEC = pl.BlockSpec(memory_space=pltpu.VMEM)
ANYSPEC = pl.BlockSpec(memory_space=pl.ANY)
HBMSPEC = pl.BlockSpec(memory_space=pltpu.HBM)
SSPEC = pl.BlockSpec(memory_space=pltpu.SMEM)


def dot(a, b, dims):
    return lax.dot_general(a, b, (dims, ((), ())), preferred_element_type=f32)


def params(mib):
    return pltpu.CompilerParams(vmem_limit_bytes=mib * MIB)


def cost(flops, size, transcendentals=0):
    return pl.CostEstimate(flops=flops, bytes_accessed=size, transcendentals=transcendentals)


def after(value, *earlier):
    return lax.optimization_barrier((value, earlier))[0]


def pack_kernel(key_ref, value_ref, rate_ref, *out_refs):
    for group, out_ref in enumerate(out_refs):
        out_ref[:, :, :DH] = key_ref[group]
        rate = -rate_ref[group].astype(f32)
        out_ref[:, :, DH:] = (rate[:, :, None] * value_ref[group].astype(f32)).astype(bf16)


def pack(keys, values, rates):
    heads = 8
    spec = pl.BlockSpec((GROUPS, heads, 64, DH), lambda i: (0, i, 0, 0))
    return pl.pallas_call(
        pack_kernel,
        grid=(16 // heads,),
        out_shape=[jax.ShapeDtypeStruct((16, 64, 2 * DH), bf16)] * GROUPS,
        in_specs=[spec, spec, pl.BlockSpec((GROUPS, heads, 64), lambda i: (0, i, 0))],
        out_specs=[pl.BlockSpec((heads, 64, 2 * DH), lambda i: (i, 0, 0))] * GROUPS,
        compiler_params=params(56),
        name="pack",
        cost_estimate=cost(1, 1),
    )(keys, values, rates)


def join_kernel(own_ref, peer_ref, queries_ref, *refs):
    out_ref = refs[-1]
    out_ref[:, :, : 2 * DH] = own_ref[...]
    out_ref[:, :, 2 * DH : 4 * DH] = peer_ref[...]
    for group in range(GROUPS):
        out_ref[:, :, (4 + group) * DH : (5 + group) * DH] = queries_ref[group]


def join(own, peer, queries, *earlier):
    heads = 8
    spec = pl.BlockSpec((heads, 64, 2 * DH), lambda i: (i, 0, 0))
    return pl.pallas_call(
        join_kernel,
        grid=(16 // heads,),
        out_shape=jax.ShapeDtypeStruct((16, 64, 6 * DH), bf16),
        in_specs=[spec, spec, pl.BlockSpec((2, heads, 64, DH), lambda i: (0, i, 0, 0))]
        + [ANYSPEC] * len(earlier),
        out_specs=pl.BlockSpec((heads, 64, 6 * DH), lambda i: (i, 0, 0)),
        compiler_params=params(56),
        name="join",
        cost_estimate=cost(1, 1),
    )(own, peer, queries, *earlier)


TILES = 2 * TOK // TILE
GRAD_SCRATCH = [
    pltpu.VMEM((3, DH, HALF), f32),
    pltpu.VMEM((TILES, TILE, 2 * DH), bf16),
    pltpu.SemaphoreType.DMA((TILES,)),
]


def token_copies(sides, kd, sem):
    copies = []
    for side, (ref, column) in enumerate(sides):
        for tile in range(TILES // 2):
            source = ref.at[pl.ds(tile * TILE, TILE), pl.ds(column, 2 * DH)]
            at = side * (TILES // 2) + tile
            copies.append(pltpu.make_async_copy(source, kd.at[at], sem.at[at]))
    return copies


def grad_body(kd, kd_sem, wb, acc_ref, out_refs, deep):
    acc_ref[...] = jnp.zeros_like(acc_ref)

    def tile(at, carry):
        pltpu.make_async_copy(kd.at[at], kd.at[at], kd_sem.at[at]).wait()
        key = kd[at, :, :DH]
        dout = kd[at, :, DH:]
        gate = dot(key, wb[0], ((1,), (0,)))
        up = dot(key, wb[1], ((1,), (0,)))
        dhid = dot(dout, wb[2], ((1,), (0,)))
        sigma = jax.nn.sigmoid(gate)
        active = gate * sigma
        hidden = (active * up).astype(bf16)
        d_up = (dhid * active).astype(bf16)
        d_gate = (dhid * up * sigma * (1.0 + gate * (1.0 - sigma))).astype(bf16)
        for index, (left, right) in enumerate(((key, d_gate), (key, d_up), (dout, hidden))):
            acc_ref[index] += dot(left, right, ((0,), (0,)))
        return carry

    lax.fori_loop(0, TILES, tile, 0)
    for far in range(4):
        cols = pl.ds(pl.multiple_of(((deep + far) & 3) * LANE, LANE), LANE)
        out_refs[far][...] = acc_ref[:, :, cols].astype(bf16)


def grad_kernel(place_ref, own_ref, peer_ref, wb_ref, *refs):
    out_refs, (acc_ref, kd, kd_sem, wb, wb_sem) = refs[:4], refs[4:]
    fetch = pltpu.make_async_copy(wb_ref.at[0], wb, wb_sem)
    fetch.start()
    copies = token_copies(((own_ref, 0), (peer_ref, 0)), kd, kd_sem)
    copies[0].start()
    fetch.wait()
    for copy in copies[1:]:
        copy.start()
    grad_body(kd, kd_sem, wb, acc_ref, out_refs, place_ref[1])


def grads(place, own, peer, both):
    return pl.pallas_call(
        grad_kernel,
        out_shape=[jax.ShapeDtypeStruct((3, DH, LANE), bf16)] * 4,
        in_specs=[SSPEC] + [HBMSPEC] * 3,
        out_specs=[VSPEC] * 4,
        scratch_shapes=GRAD_SCRATCH + [pltpu.VMEM((3, DH, HALF), bf16), pltpu.SemaphoreType.DMA(())],
        compiler_params=params(24),
        name="grads",
        cost_estimate=cost(12 * 2 * TOK * DH * HALF, 4 * MIB, 2 * TOK * HALF),
    )(place, own, peer, both)


NS_SCRATCH = [
    pltpu.VMEM((3, DH, FF), bf16),
    pltpu.VMEM((3, 8, DH, LANE), f32),
    pltpu.VMEM((2, 3, DH, HALF), bf16),
    pltpu.SemaphoreType.DMA(()),
]


def renew(weight, value, step):
    cand = weight - step * value.astype(f32)
    scale = jnp.sqrt(jnp.sum(weight * weight, axis=0, keepdims=True) + 1e-06) / jnp.sqrt(
        jnp.sum(cand * cand, axis=0, keepdims=True) + 1e-06
    )
    return cand * scale


def ns_body(grad, w_ref, step_ref, scratch, others, keep):
    ortho, weights, both, sem = scratch
    fetch = pltpu.make_async_copy(w_ref, weights, sem)
    fetch.start()
    for other in others:
        other.start()
    def begin(index, carry):
        total = None
        for half in range(2):
            for chunk in range(4):
                part = grad[half, chunk, index].astype(f32)
                part = part * part
                total = part if total is None else total + part
        total = jnp.sum(jnp.sum(total, axis=0, keepdims=True), axis=1, keepdims=True)
        norm = jnp.sqrt(total) + 1e-07
        for half in range(2):
            for chunk in range(4):
                at = (half * 4 + chunk) * LANE
                unit = (grad[half, chunk, index].astype(f32) / norm).astype(bf16)
                ortho[index, :, at : at + LANE] = unit
        return carry

    def iterate(step, carry):
        grams = [dot(ortho[i], ortho[i], ((1,), (1,))).astype(bf16) for i in range(3)]
        squares = [dot(gram, gram, ((1,), (0,))) for gram in grams]
        polys = [
            (coef_b * gram.astype(f32) + coef_c * square).astype(bf16) for gram, square in zip(grams, squares)
        ]
        for i in range(3):
            moved = dot(polys[i], ortho[i], ((1,), (0,)))
            ortho[i] = (coef_a * ortho[i].astype(f32) + moved).astype(bf16)
        return carry

    def update(index, carry):
        step = step_ref[0:1, 0:1]
        for chunk in range(8):
            value = ortho[index, :, chunk * LANE : (chunk + 1) * LANE]
            fresh = renew(weights[index, chunk], value, step)
            at = (chunk % 4) * LANE
            both[chunk // 4, index, :, at : at + LANE] = fresh.astype(bf16)
            if keep:
                weights[index, chunk] = fresh
        return carry

    lax.fori_loop(0, 3, begin, 0)
    lax.fori_loop(0, NS_STEPS, iterate, 0, unroll=True)
    fetch.wait()
    lax.fori_loop(0, 3, update, 0)


NS_FLOPS = 3 * 1510 * 10**6
BOTH = jax.ShapeDtypeStruct((2, 3, DH, HALF), bf16)


GRAD_PIECES = [pltpu.VMEM((2, 4, 3, DH, LANE), bf16), pltpu.SemaphoreType.DMA((8,))]


def load_pieces(g_refs, grad, sem, deep):
    pieces = []
    for i, ref in enumerate(g_refs):
        if len(g_refs) == 2:
            target = grad.at[i]
        else:
            target = grad.at[i // 4, (deep + i) & 3]
        pieces.append(pltpu.make_async_copy(ref, target, sem.at[i]))
    for piece in pieces:
        piece.start()
    for piece in pieces:
        piece.wait()
    return grad


def turn_kernel(*refs):
    place_ref, g_refs, w_ref, step_ref, rest_ref = refs[0], refs[1:3], *refs[3:6]
    both_ref, wnew_ref, out_refs, scratch = refs[6], refs[7], refs[8:12], refs[12:]
    ns_scratch, (acc_ref, kd, kd_sem), sem = scratch[:4], scratch[4:7], scratch[7]
    weights, both = ns_scratch[1], ns_scratch[2]
    grad = load_pieces(g_refs, *scratch[8:], place_ref[1])
    copies = token_copies(((rest_ref, 0), (rest_ref, 2 * DH)), kd, kd_sem)
    ns_body(grad, w_ref, step_ref, ns_scratch, copies, True)
    done = [
        pltpu.make_async_copy(both, both_ref, sem.at[0]),
        pltpu.make_async_copy(weights, wnew_ref, sem.at[1]),
    ]
    for copy in done:
        copy.start()
    grad_body(kd, kd_sem, both.at[0], acc_ref, out_refs, place_ref[1])
    for copy in done:
        copy.wait()


def turn(place, chunks, weight, step, rest):
    return pl.pallas_call(
        turn_kernel,
        out_shape=[BOTH, jax.ShapeDtypeStruct((3, 8, DH, LANE), f32)]
        + [jax.ShapeDtypeStruct((3, DH, LANE), bf16)] * 4,
        in_specs=[SSPEC] + [HBMSPEC] * 3 + [VSPEC, HBMSPEC],
        out_specs=[HBMSPEC] * 2 + [VSPEC] * 4,
        scratch_shapes=NS_SCRATCH + GRAD_SCRATCH + [pltpu.SemaphoreType.DMA((2,))] + GRAD_PIECES,
        compiler_params=params(56),
        name="turn",
        cost_estimate=cost(NS_FLOPS + 12 * 2 * TOK * DH * HALF, 14 * MIB, 2 * TOK * HALF),
    )(place, *chunks, weight, step, rest)


def query_half(queries, weights, half, acc_ref, out_ref, column):
    def tile(at, carry):
        rows = pl.ds(pl.multiple_of(at * TILE, TILE), TILE)
        query = queries[rows, :]
        gate = dot(query, weights[0], ((1,), (0,)))
        up = dot(query, weights[1], ((1,), (0,)))
        hidden = (gate * jax.nn.sigmoid(gate) * up).astype(bf16)
        part = dot(hidden, weights[2], ((1,), (1,)))
        if half:
            out_ref[rows, column : column + DH] = (acc_ref[rows, :] + part).astype(bf16)
        else:
            acc_ref[rows, :] = part
        return carry

    lax.fori_loop(0, TOK // TILE, tile, 0, unroll=True)


QUERY_SCRATCH = [pltpu.VMEM((TOK, DH), f32), pltpu.VMEM((TOK, DH), bf16), pltpu.SemaphoreType.DMA(())]


def query_kernel(column, rest_ref, both_ref, *refs):
    out_ref, acc_ref, queries, q_sem, both, sem = refs[-6:]
    copies = [pltpu.make_async_copy(both_ref.at[half], both.at[half], sem.at[half]) for half in range(2)]
    fetch = pltpu.make_async_copy(rest_ref.at[:, pl.ds(column, DH)], queries, q_sem)
    fetch.start()
    copies[0].start()
    fetch.wait()
    copies[0].wait()
    copies[1].start()
    query_half(queries, both.at[0], 0, acc_ref, out_ref, 0)
    copies[1].wait()
    query_half(queries, both.at[1], 1, acc_ref, out_ref, 0)


def forward(rest, both, column, *earlier):
    return pl.pallas_call(
        functools.partial(query_kernel, column),
        out_shape=jax.ShapeDtypeStruct((TOK, DH), bf16),
        in_specs=[HBMSPEC] * 2 + [ANYSPEC] * len(earlier),
        out_specs=VSPEC,
        scratch_shapes=QUERY_SCRATCH + [pltpu.VMEM((2, 3, DH, HALF), bf16), pltpu.SemaphoreType.DMA((2,))],
        compiler_params=params(56),
        name="forward",
        cost_estimate=cost(6 * TOK * DH * FF, 3 * MIB, TOK * FF),
    )(rest, both, *earlier)


def close_kernel(*refs):
    place_ref, g_refs, w_ref, step_ref, rest_ref = refs[0], refs[1:9], *refs[9:12]
    one_ref, two_ref, out_ref = refs[-13:-10]
    ns_scratch, pieces, (acc_ref, queries, q_sem), sem = refs[-10:-6], refs[-6:-4], refs[-4:-1], refs[-1]
    both = ns_scratch[2]
    fetch = pltpu.make_async_copy(rest_ref.at[:, pl.ds(5 * DH, DH)], queries, q_sem)
    ns_body(load_pieces(g_refs, *pieces, place_ref[1]), w_ref, step_ref, ns_scratch, [fetch], False)
    done = [
        pltpu.make_async_copy(both.at[0], one_ref, sem.at[0]),
        pltpu.make_async_copy(both.at[1], two_ref, sem.at[1]),
    ]
    for copy in done:
        copy.start()
    fetch.wait()
    for half in range(2):
        query_half(queries, both.at[half], half, acc_ref, out_ref, 0)
    for copy in done:
        copy.wait()


def close(place, chunks, weight, step, rest, *earlier):
    return pl.pallas_call(
        close_kernel,
        out_shape=[jax.ShapeDtypeStruct((3, DH, HALF), bf16)] * 2 + [jax.ShapeDtypeStruct((TOK, DH), bf16)],
        in_specs=[SSPEC] + [HBMSPEC] * 9 + [VSPEC, HBMSPEC] + [ANYSPEC] * len(earlier),
        out_specs=[HBMSPEC, HBMSPEC, VSPEC],
        scratch_shapes=NS_SCRATCH + GRAD_PIECES + QUERY_SCRATCH + [pltpu.SemaphoreType.DMA((2,))],
        compiler_params=params(56),
        name="close",
        cost_estimate=cost(NS_FLOPS + 6 * TOK * DH * FF, 10 * MIB, TOK * FF),
    )(place, *chunks, weight, step, rest, *earlier)


def prep_kernel(place_ref, *refs):
    local, other, step_ref, step_other_ref = refs[:3], refs[3:6], refs[6], refs[7]
    wrot_ref, both_ref, step_out_ref, weights, sem, out_sem = refs[8:]
    core, mine, row = place_ref[0], place_ref[2], place_ref[3]
    step_out_ref[...] = jnp.where(mine == 1, step_ref[...], step_other_ref[...])

    def fetch(sources):
        copies = []
        for index in range(3):
            for chunk in range(8):
                block = (core ^ (chunk // 4)) * 4 + chunk % 4
                cols = pl.ds(pl.multiple_of(block * LANE, LANE), LANE)
                copies.append(
                    pltpu.make_async_copy(
                        sources[index].at[row, :, cols], weights.at[index, chunk], sem.at[index, chunk]
                    )
                )
        return copies

    @pl.when(mine == 1)
    def _():
        for copy in fetch(local):
            copy.start()

    @pl.when(mine != 1)
    def _():
        for copy in fetch(other):
            copy.start()

    def cast(index, carry):
        for chunk in range(8):
            pltpu.make_async_copy(weights.at[index, chunk], weights.at[index, chunk], sem.at[index, chunk]).wait()
            at = (chunk % 4) * LANE
            both_ref[chunk // 4, index, :, at : at + LANE] = weights[index, chunk].astype(bf16)
        return carry

    lax.fori_loop(0, 3, cast, 0)
    copy = pltpu.make_async_copy(weights, wrot_ref, out_sem)
    copy.start()
    copy.wait()


def prepare(place, local, other, step, step_other):
    return pl.pallas_call(
        prep_kernel,
        out_shape=(
            jax.ShapeDtypeStruct((3, 8, DH, LANE), f32),
            BOTH,
            jax.ShapeDtypeStruct((8, LANE), f32),
        ),
        in_specs=[SSPEC] + [HBMSPEC] * 6 + [VSPEC] * 2,
        out_specs=(HBMSPEC, VSPEC, VSPEC),
        scratch_shapes=[
            pltpu.VMEM((3, 8, DH, LANE), f32),
            pltpu.SemaphoreType.DMA((3, 8)),
            pltpu.SemaphoreType.DMA(()),
        ],
        compiler_params=params(56),
        name="prepare",
        cost_estimate=cost(1, 1),
    )(place, *local, *other, step, step_other)


def final_kernel(place_ref, *refs):
    near, sent, outs, result_ref = refs[:8], refs[8:10], refs[10:13], refs[13]
    buf, wide, late, wide_late, in_sem, out_sem, late_sem, result_sem = refs[14:]
    core, row = place_ref[0], place_ref[4]
    slots = [(head, half) for head in range(2) for half in range(2)]
    fetches = [pltpu.make_async_copy(sent[i], late.at[i], late_sem.at[i]) for i in range(GROUPS)]
    for fetch in fetches:
        fetch.start()

    def start(ref, slot):
        pltpu.make_async_copy(ref, buf.at[slot], in_sem.at[slot]).start()

    for slot, (head, half) in enumerate(slots):
        away = (row - 2 * core - head) & 3
        flip = core ^ half
        for far in range(4):
            for side in range(2):
                pl.when((away == far) & (flip == side))(functools.partial(start, near[2 * far + side], slot))
    done = []
    for group in range(GROUPS):
        fetches[group].wait()
        wide_late[group] = late[group].astype(f32)
        done.append(pltpu.make_async_copy(wide_late.at[group], result_ref.at[group], result_sem.at[group]))
        done[-1].start()

    def write(slot, carry):
        head, half = slot // 2, slot % 2
        pltpu.make_async_copy(buf.at[slot], buf.at[slot], in_sem.at[slot]).wait()
        for index in range(3):
            wide[slot, index] = buf[slot, index].astype(f32)
            cols = pl.ds(pl.multiple_of(half * HALF, HALF), HALF)
            target = outs[index].at[head, :, cols]
            pltpu.make_async_copy(wide.at[slot, index], target, out_sem.at[slot, index]).start()
        return carry

    lax.fori_loop(0, 4, write, 0)
    for slot, (head, half) in enumerate(slots):
        for index in range(3):
            target = outs[index].at[head, :, pl.ds(half * HALF, HALF)]
            done.append(pltpu.make_async_copy(wide.at[slot, index], target, out_sem.at[slot, index]))
    for copy in done:
        copy.wait()


def finish(place, near, sent):
    return pl.pallas_call(
        final_kernel,
        out_shape=[jax.ShapeDtypeStruct((2, DH, FF), f32)] * 3
        + [jax.ShapeDtypeStruct((GROUPS, 16, 64, DH), f32)],
        in_specs=[SSPEC] + [HBMSPEC] * 10,
        out_specs=[HBMSPEC] * 4,
        scratch_shapes=[
            pltpu.VMEM((4, 3, DH, HALF), bf16),
            pltpu.VMEM((4, 3, DH, HALF), f32),
            pltpu.VMEM((GROUPS, 16, 64, DH), bf16),
            pltpu.VMEM((GROUPS, 16, 64, DH), f32),
            pltpu.SemaphoreType.DMA((4,)),
            pltpu.SemaphoreType.DMA((4, 3)),
            pltpu.SemaphoreType.DMA((GROUPS,)),
            pltpu.SemaphoreType.DMA((GROUPS,)),
        ],
        compiler_params=params(56),
        name="finish",
        cost_estimate=cost(10**6, 15 * MIB),
    )(place, *near, *sent)


def ring(far):
    return [(i, (i + far) % 4) for i in range(4)]


SWAP = [(0, 1), (1, 0)]


def swap(value):
    return lax.ppermute(value, "c", SWAP)


def sum_up(partial):
    received = [lax.ppermute(partial[far], "z", ring(far)) for far in (2, 1, 3)]
    total = partial[0].astype(f32)
    for part in received:
        total = total + part.astype(f32)
    return total.astype(bf16)


def gather(value):
    whole = lax.all_gather(value, "z")
    return whole, swap(whole)


def gather_direct(value):
    far2, far1, far3 = [lax.ppermute(value, "z", ring(4 - far)) for far in (2, 1, 3)]
    chunks = [value, far1, far2, far3]
    return chunks + [swap(chunk) for chunk in chunks]


def y_pairs(start, end):
    return [(2 * ((y + start) % 4) + y // 2, 2 * ((y + end) % 4) + y // 2) for y in range(4)]


def shards(queries, keys, values, rates, step_sizes, w_gate, w_up, w_down):
    z, y, c = lax.axis_index("z"), lax.axis_index("y"), lax.axis_index("c")
    exchange = functools.partial(
        lax.all_to_all, axis_name=("x", "y"), split_axis=0, concat_axis=0, tiled=True
    )
    packed, own = pack(keys, values, rates)
    first = exchange(packed).reshape(TOK, 2 * DH)
    mine = (c == y // 2).astype(jnp.int32)
    stored = (w_gate, w_up, w_down)
    step_local = jnp.broadcast_to(lax.dynamic_index_in_dim(step_sizes, y % 2, 0), (8, LANE))
    place = jnp.stack([c, z, mine, y % 2, y]).astype(jnp.int32)
    others = [swap(w) for w in stored]
    weights, both, step = prepare(place, stored, others, step_local, swap(step_local))
    second = join(own, swap(own), queries, step)
    first = after(first, step, second)
    rest = exchange(after(second, first)).reshape(TOK, 6 * DH)

    chunks = gather(sum_up(grads(place, first, swap(first), both)))
    both, weights, *partial = turn(place, chunks, weights, step, rest)

    early = exchange(forward(rest, both, 4 * DH, partial[0]).reshape(16, 64, DH))
    chunks = gather_direct(sum_up(partial))
    one, two, result = close(place, chunks, weights, step, rest, early)
    move = functools.partial(lax.ppermute, axis_name=("y", "c"))
    up, down = move(one, perm=y_pairs(0, 1)), move(two, perm=y_pairs(0, 3))
    near = [one, two, up, move(two, perm=y_pairs(0, 1))]
    near += [move(up, perm=y_pairs(1, 2)), move(down, perm=y_pairs(3, 2))]
    near += [move(one, perm=y_pairs(0, 3)), down]
    late = exchange(result.reshape(16, 64, DH))
    gate, up, down, outputs = finish(place, near, (early, late))
    return (outputs, gate, up, down)


def solution(mesh):
    grid = Mesh(mesh.devices.reshape(4, 4, 4, 2), ("z", "y", "x", "c"))
    tokens = ("z", "y", "x", "c")
    heads = ("x", "c")
    return jax.shard_map(
        shards,
        mesh=grid,
        in_specs=(
            P(None, None, tokens, None),
            P(None, None, tokens, None),
            P(None, None, tokens, None),
            P(None, None, tokens),
            P(heads),
            P(heads, None, None),
            P(heads, None, None),
            P(heads, None, None),
        ),
        out_specs=(
            P(None, None, tokens, None),
            P(heads, None, None),
            P(heads, None, None),
            P(heads, None, None),
        ),
        check_vma=False,
    )
```

```python
import functools

import jax
import jax.numpy as jnp
from jax import lax
from jax.experimental import pallas as pl
from jax.experimental.pallas import tpu as pltpu
from jax.sharding import Mesh
from jax.sharding import PartitionSpec as P

GROUPS = 2
NS_STEPS = 5
DH = 256
FF = 1024
HALF = FF // 2
LANE = 128
TOK = 1024
TILE = 512

coef_a = 3.4445
coef_b = -4.775
coef_c = 2.0315

f32 = jnp.float32
bf16 = jnp.bfloat16
MIB = 1024 * 1024

VSPEC = pl.BlockSpec(memory_space=pltpu.VMEM)
ANYSPEC = pl.BlockSpec(memory_space=pl.ANY)
HBMSPEC = pl.BlockSpec(memory_space=pltpu.HBM)
SSPEC = pl.BlockSpec(memory_space=pltpu.SMEM)


def dot(a, b, dims):
    return lax.dot_general(a, b, (dims, ((), ())), preferred_element_type=f32)


def params(mib):
    return pltpu.CompilerParams(vmem_limit_bytes=mib * MIB)


def cost(flops, size, transcendentals=0):
    return pl.CostEstimate(flops=flops, bytes_accessed=size, transcendentals=transcendentals)


def after(value, *earlier):
    return lax.optimization_barrier((value, earlier))[0]


def pack_kernel(key_ref, value_ref, rate_ref, *out_refs):
    for group, out_ref in enumerate(out_refs):
        out_ref[:, :, :DH] = key_ref[group]
        rate = -rate_ref[group].astype(f32)
        out_ref[:, :, DH:] = (rate[:, :, None] * value_ref[group].astype(f32)).astype(bf16)


def pack(keys, values, rates):
    heads = 8
    spec = pl.BlockSpec((GROUPS, heads, 64, DH), lambda i: (0, i, 0, 0))
    return pl.pallas_call(
        pack_kernel,
        grid=(16 // heads,),
        out_shape=[jax.ShapeDtypeStruct((16, 64, 2 * DH), bf16)] * GROUPS,
        in_specs=[spec, spec, pl.BlockSpec((GROUPS, heads, 64), lambda i: (0, i, 0))],
        out_specs=[pl.BlockSpec((heads, 64, 2 * DH), lambda i: (i, 0, 0))] * GROUPS,
        compiler_params=params(56),
        name="pack",
        cost_estimate=cost(1, 1),
    )(keys, values, rates)


def join_kernel(own_ref, peer_ref, queries_ref, *refs):
    out_ref = refs[-1]
    out_ref[:, :, : 2 * DH] = own_ref[...]
    out_ref[:, :, 2 * DH : 4 * DH] = peer_ref[...]
    for group in range(GROUPS):
        out_ref[:, :, (4 + group) * DH : (5 + group) * DH] = queries_ref[group]


def join(own, peer, queries, *earlier):
    heads = 8
    spec = pl.BlockSpec((heads, 64, 2 * DH), lambda i: (i, 0, 0))
    return pl.pallas_call(
        join_kernel,
        grid=(16 // heads,),
        out_shape=jax.ShapeDtypeStruct((16, 64, 6 * DH), bf16),
        in_specs=[spec, spec, pl.BlockSpec((2, heads, 64, DH), lambda i: (0, i, 0, 0))]
        + [ANYSPEC] * len(earlier),
        out_specs=pl.BlockSpec((heads, 64, 6 * DH), lambda i: (i, 0, 0)),
        compiler_params=params(56),
        name="join",
        cost_estimate=cost(1, 1),
    )(own, peer, queries, *earlier)


TILES = 2 * TOK // TILE
GRAD_SCRATCH = [
    pltpu.VMEM((3, DH, HALF), f32),
    pltpu.VMEM((TILES, TILE, 2 * DH), bf16),
    pltpu.SemaphoreType.DMA((TILES,)),
]


def token_copies(sides, kd, sem):
    copies = []
    for side, (ref, column) in enumerate(sides):
        for tile in range(TILES // 2):
            source = ref.at[pl.ds(tile * TILE, TILE), pl.ds(column, 2 * DH)]
            at = side * (TILES // 2) + tile
            copies.append(pltpu.make_async_copy(source, kd.at[at], sem.at[at]))
    return copies


def grad_body(kd, kd_sem, wb, acc_ref, out_refs, deep):
    acc_ref[...] = jnp.zeros_like(acc_ref)

    def tile(at, carry):
        pltpu.make_async_copy(kd.at[at], kd.at[at], kd_sem.at[at]).wait()
        key = kd[at, :, :DH]
        dout = kd[at, :, DH:]
        gate = dot(key, wb[0], ((1,), (0,)))
        up = dot(key, wb[1], ((1,), (0,)))
        dhid = dot(dout, wb[2], ((1,), (0,)))
        sigma = 0.5 * jnp.tanh(0.5 * gate) + 0.5
        active = gate * sigma
        hidden = (active * up).astype(bf16)
        d_up = (dhid * active).astype(bf16)
        d_gate = (dhid * up * (sigma + active * (1.0 - sigma))).astype(bf16)
        for index, (left, right) in enumerate(((key, d_gate), (key, d_up), (dout, hidden))):
            acc_ref[index] += dot(left, right, ((0,), (0,)))
        return carry

    lax.fori_loop(0, TILES, tile, 0)
    for far in range(4):
        cols = pl.ds(pl.multiple_of(((deep + far) & 3) * LANE, LANE), LANE)
        out_refs[far][...] = acc_ref[:, :, cols].astype(bf16)


def grad_kernel(place_ref, own_ref, peer_ref, wb_ref, *refs):
    out_refs, (acc_ref, kd, kd_sem, wb, wb_sem) = refs[:4], refs[4:]
    fetch = pltpu.make_async_copy(wb_ref.at[0], wb, wb_sem)
    fetch.start()
    copies = token_copies(((own_ref, 0), (peer_ref, 0)), kd, kd_sem)
    copies[0].start()
    fetch.wait()
    for copy in copies[1:]:
        copy.start()
    grad_body(kd, kd_sem, wb, acc_ref, out_refs, place_ref[1])


def grads(place, own, peer, both):
    return pl.pallas_call(
        grad_kernel,
        out_shape=[jax.ShapeDtypeStruct((3, DH, LANE), bf16)] * 4,
        in_specs=[SSPEC] + [HBMSPEC] * 3,
        out_specs=[VSPEC] * 4,
        scratch_shapes=GRAD_SCRATCH + [pltpu.VMEM((3, DH, HALF), bf16), pltpu.SemaphoreType.DMA(())],
        compiler_params=params(24),
        name="grads",
        cost_estimate=cost(12 * 2 * TOK * DH * HALF, 4 * MIB, 2 * TOK * HALF),
    )(place, own, peer, both)


NS_SCRATCH = [
    pltpu.VMEM((3, DH, FF), bf16),
    pltpu.VMEM((3, 8, DH, LANE), f32),
    pltpu.VMEM((2, 3, DH, HALF), bf16),
    pltpu.SemaphoreType.DMA(()),
]


def renew(weight, value, step):
    cand = weight - step * value.astype(f32)
    scale = jnp.sqrt(jnp.sum(weight * weight, axis=0, keepdims=True) + 1e-06) / jnp.sqrt(
        jnp.sum(cand * cand, axis=0, keepdims=True) + 1e-06
    )
    return cand * scale


def ns_body(grad, w_ref, step_ref, scratch, others, keep):
    ortho, weights, both, sem = scratch
    fetch = pltpu.make_async_copy(w_ref, weights, sem)
    fetch.start()
    for other in others:
        other.start()
    def begin(index, carry):
        total = None
        for half in range(2):
            for chunk in range(4):
                part = grad[half, chunk, index].astype(f32)
                part = part * part
                total = part if total is None else total + part
        total = jnp.sum(jnp.sum(total, axis=0, keepdims=True), axis=1, keepdims=True)
        norm = jnp.sqrt(total) + 1e-07
        for half in range(2):
            for chunk in range(4):
                at = (half * 4 + chunk) * LANE
                unit = (grad[half, chunk, index].astype(f32) / norm).astype(bf16)
                ortho[index, :, at : at + LANE] = unit
        return carry

    def iterate(step, carry):
        grams = [dot(ortho[i], ortho[i], ((1,), (1,))).astype(bf16) for i in range(3)]
        squares = [dot(gram, gram, ((1,), (0,))) for gram in grams]
        polys = [
            (coef_b * gram.astype(f32) + coef_c * square).astype(bf16) for gram, square in zip(grams, squares)
        ]
        for i in range(3):
            moved = dot(polys[i], ortho[i], ((1,), (0,)))
            ortho[i] = (coef_a * ortho[i].astype(f32) + moved).astype(bf16)
        return carry

    def update(index, carry):
        step = step_ref[0:1, 0:1]
        for chunk in range(8):
            value = ortho[index, :, chunk * LANE : (chunk + 1) * LANE]
            fresh = renew(weights[index, chunk], value, step)
            at = (chunk % 4) * LANE
            both[chunk // 4, index, :, at : at + LANE] = fresh.astype(bf16)
            if keep:
                weights[index, chunk] = fresh
        return carry

    lax.fori_loop(0, 3, begin, 0)
    lax.fori_loop(0, NS_STEPS, iterate, 0, unroll=True)
    fetch.wait()
    lax.fori_loop(0, 3, update, 0)


NS_FLOPS = 3 * 1510 * 10**6
BOTH = jax.ShapeDtypeStruct((2, 3, DH, HALF), bf16)


GRAD_PIECES = [pltpu.VMEM((2, 4, 3, DH, LANE), bf16), pltpu.SemaphoreType.DMA((8,))]


def load_pieces(g_refs, grad, sem, deep):
    pieces = []
    for i, ref in enumerate(g_refs):
        if len(g_refs) == 2:
            target = grad.at[i]
        else:
            target = grad.at[i // 4, (deep + i) & 3]
        pieces.append(pltpu.make_async_copy(ref, target, sem.at[i]))
    for piece in pieces:
        piece.start()
    for piece in pieces:
        piece.wait()
    return grad


def turn_kernel(*refs):
    place_ref, g_refs, w_ref, step_ref, rest_ref = refs[0], refs[1:3], *refs[3:6]
    both_ref, wnew_ref, out_refs, scratch = refs[6], refs[7], refs[8:12], refs[12:]
    ns_scratch, (acc_ref, kd, kd_sem), sem = scratch[:4], scratch[4:7], scratch[7]
    weights, both = ns_scratch[1], ns_scratch[2]
    grad = load_pieces(g_refs, *scratch[8:], place_ref[1])
    copies = token_copies(((rest_ref, 0), (rest_ref, 2 * DH)), kd, kd_sem)
    ns_body(grad, w_ref, step_ref, ns_scratch, copies, True)
    done = [
        pltpu.make_async_copy(both, both_ref, sem.at[0]),
        pltpu.make_async_copy(weights, wnew_ref, sem.at[1]),
    ]
    for copy in done:
        copy.start()
    grad_body(kd, kd_sem, both.at[0], acc_ref, out_refs, place_ref[1])
    for copy in done:
        copy.wait()


def turn(place, chunks, weight, step, rest):
    return pl.pallas_call(
        turn_kernel,
        out_shape=[BOTH, jax.ShapeDtypeStruct((3, 8, DH, LANE), f32)]
        + [jax.ShapeDtypeStruct((3, DH, LANE), bf16)] * 4,
        in_specs=[SSPEC] + [ANYSPEC] * 2 + [HBMSPEC, VSPEC, HBMSPEC],
        out_specs=[HBMSPEC] * 2 + [VSPEC] * 4,
        scratch_shapes=NS_SCRATCH + GRAD_SCRATCH + [pltpu.SemaphoreType.DMA((2,))] + GRAD_PIECES,
        compiler_params=params(56),
        name="turn",
        cost_estimate=cost(NS_FLOPS + 12 * 2 * TOK * DH * HALF, 14 * MIB, 2 * TOK * HALF),
    )(place, *chunks, weight, step, rest)


def query_half(queries, weights, half, acc_ref, out_ref, column):
    def tile(at, carry):
        rows = pl.ds(pl.multiple_of(at * TILE, TILE), TILE)
        query = queries[rows, :]
        gate = dot(query, weights[0], ((1,), (0,)))
        up = dot(query, weights[1], ((1,), (0,)))
        hidden = (gate * (0.5 * jnp.tanh(0.5 * gate) + 0.5) * up).astype(bf16)
        part = dot(hidden, weights[2], ((1,), (1,)))
        if half:
            out_ref[rows, column : column + DH] = (acc_ref[rows, :] + part).astype(bf16)
        else:
            acc_ref[rows, :] = part
        return carry

    lax.fori_loop(0, TOK // TILE, tile, 0, unroll=True)


QUERY_SCRATCH = [pltpu.VMEM((TOK, DH), f32), pltpu.VMEM((TOK, DH), bf16), pltpu.SemaphoreType.DMA(())]


def query_kernel(column, rest_ref, both_ref, *refs):
    out_ref, acc_ref, queries, q_sem, both, sem = refs[-6:]
    copies = [pltpu.make_async_copy(both_ref.at[half], both.at[half], sem.at[half]) for half in range(2)]
    fetch = pltpu.make_async_copy(rest_ref.at[:, pl.ds(column, DH)], queries, q_sem)
    fetch.start()
    copies[0].start()
    fetch.wait()
    copies[0].wait()
    copies[1].start()
    query_half(queries, both.at[0], 0, acc_ref, out_ref, 0)
    copies[1].wait()
    query_half(queries, both.at[1], 1, acc_ref, out_ref, 0)


def forward(rest, both, column, *earlier):
    return pl.pallas_call(
        functools.partial(query_kernel, column),
        out_shape=jax.ShapeDtypeStruct((TOK, DH), bf16),
        in_specs=[HBMSPEC] * 2 + [ANYSPEC] * len(earlier),
        out_specs=VSPEC,
        scratch_shapes=QUERY_SCRATCH + [pltpu.VMEM((2, 3, DH, HALF), bf16), pltpu.SemaphoreType.DMA((2,))],
        compiler_params=params(56),
        name="forward",
        cost_estimate=cost(6 * TOK * DH * FF, 3 * MIB, TOK * FF),
    )(rest, both, *earlier)


def close_kernel(*refs):
    place_ref, g_refs, w_ref, step_ref, rest_ref = refs[0], refs[1:9], *refs[9:12]
    both_ref, quarter_ref, out_ref = refs[-14:-11]
    ns_scratch, pieces, (acc_ref, queries, q_sem), (quarter, sem) = refs[-11:-7], refs[-7:-5], refs[-5:-2], refs[-2:]
    both = ns_scratch[2]
    fetch = pltpu.make_async_copy(rest_ref.at[:, pl.ds(5 * DH, DH)], queries, q_sem)
    ns_body(load_pieces(g_refs, *pieces, place_ref[1]), w_ref, step_ref, ns_scratch, [fetch], False)
    cols = pl.ds(pl.multiple_of(place_ref[1] * LANE, LANE), LANE)
    for half in range(2):
        quarter[half] = both[half, :, :, cols]
    done = [
        pltpu.make_async_copy(quarter, quarter_ref, sem.at[0]),
        pltpu.make_async_copy(both, both_ref, sem.at[1]),
    ]
    for copy in done:
        copy.start()
    fetch.wait()
    for half in range(2):
        query_half(queries, both.at[half], half, acc_ref, out_ref, 0)
    for copy in done:
        copy.wait()


def close(place, chunks, weight, step, rest, *earlier):
    return pl.pallas_call(
        close_kernel,
        out_shape=[
            BOTH,
            jax.ShapeDtypeStruct((2, 3, DH, LANE), bf16),
            jax.ShapeDtypeStruct((TOK, DH), bf16),
        ],
        in_specs=[SSPEC] + [ANYSPEC] * 8 + [HBMSPEC, VSPEC, HBMSPEC] + [ANYSPEC] * len(earlier),
        out_specs=[HBMSPEC, HBMSPEC, VSPEC],
        scratch_shapes=NS_SCRATCH
        + GRAD_PIECES
        + QUERY_SCRATCH
        + [pltpu.VMEM((2, 3, DH, LANE), bf16), pltpu.SemaphoreType.DMA((2,))],
        compiler_params=params(56),
        name="close",
        cost_estimate=cost(NS_FLOPS + 6 * TOK * DH * FF, 10 * MIB, TOK * FF),
    )(place, *chunks, weight, step, rest, *earlier)


def prep_kernel(place_ref, *refs):
    local, other, step_ref, step_other_ref = refs[:3], refs[3:6], refs[6], refs[7]
    wrot_ref, both_ref, step_out_ref, weights, sem, out_sem = refs[8:]
    core, mine, row = place_ref[0], place_ref[2], place_ref[3]
    step_out_ref[...] = jnp.where(mine == 1, step_ref[...], step_other_ref[...])

    def fetch(sources):
        copies = []
        for index in range(3):
            for chunk in range(8):
                block = (core ^ (chunk // 4)) * 4 + chunk % 4
                cols = pl.ds(pl.multiple_of(block * LANE, LANE), LANE)
                copies.append(
                    pltpu.make_async_copy(
                        sources[index].at[row, :, cols], weights.at[index, chunk], sem.at[index, chunk]
                    )
                )
        return copies

    @pl.when(mine == 1)
    def _():
        for copy in fetch(local):
            copy.start()

    @pl.when(mine != 1)
    def _():
        for copy in fetch(other):
            copy.start()

    def cast(index, carry):
        for chunk in range(8):
            pltpu.make_async_copy(weights.at[index, chunk], weights.at[index, chunk], sem.at[index, chunk]).wait()
            at = (chunk % 4) * LANE
            both_ref[chunk // 4, index, :, at : at + LANE] = weights[index, chunk].astype(bf16)
        return carry

    lax.fori_loop(0, 3, cast, 0)
    copy = pltpu.make_async_copy(weights, wrot_ref, out_sem)
    copy.start()
    copy.wait()


def prepare(place, local, other, step, step_other):
    return pl.pallas_call(
        prep_kernel,
        out_shape=(
            jax.ShapeDtypeStruct((3, 8, DH, LANE), f32),
            BOTH,
            jax.ShapeDtypeStruct((8, LANE), f32),
        ),
        in_specs=[SSPEC] + [HBMSPEC] * 6 + [VSPEC] * 2,
        out_specs=(HBMSPEC, VSPEC, VSPEC),
        scratch_shapes=[
            pltpu.VMEM((3, 8, DH, LANE), f32),
            pltpu.SemaphoreType.DMA((3, 8)),
            pltpu.SemaphoreType.DMA(()),
        ],
        compiler_params=params(56),
        name="prepare",
        cost_estimate=cost(1, 1),
    )(place, *local, *other, step, step_other)


def final_kernel(place_ref, *refs):
    near, opposite, sent, outs, result_ref = refs[:3], refs[3:7], refs[7:9], refs[9:12], refs[12]
    buf, wide, late, wide_late, in_sem, out_sem, late_sem, result_sem = refs[13:]
    core, deep, row = place_ref[0], place_ref[1], place_ref[4]
    slots = [(head, half) for head in range(2) for half in range(2)]
    fetches = [pltpu.make_async_copy(sent[i], late.at[i], late_sem.at[i]) for i in range(GROUPS)]
    for fetch in fetches:
        fetch.start()

    def straight(ref, slot, flip):
        pltpu.make_async_copy(ref.at[flip], buf.at[slot], in_sem.at[slot]).start()

    def pieces(slot, flip):
        for far in range(4):
            cols = pl.ds(pl.multiple_of(((deep + far) & 3) * LANE, LANE), LANE)
            source = opposite[far].at[1 - flip]
            pltpu.make_async_copy(source, buf.at[slot, :, :, cols], in_sem.at[slot]).start()

    for slot, (head, half) in enumerate(slots):
        away = (row - 2 * core - head) & 3
        flip = core ^ half
        for at, far in enumerate((0, 1, 3)):
            pl.when(away == far)(functools.partial(straight, near[at], slot, flip))
        pl.when(away == 2)(functools.partial(pieces, slot, flip))
    done = []
    for group in range(GROUPS):
        fetches[group].wait()
        wide_late[group] = late[group].astype(f32)
        done.append(pltpu.make_async_copy(wide_late.at[group], result_ref.at[group], result_sem.at[group]))
        done[-1].start()
    def write(slot, carry):
        head, half = slot // 2, slot % 2
        pltpu.make_async_copy(buf.at[slot], buf.at[slot], in_sem.at[slot]).wait()
        for index in range(3):
            wide[slot, index] = buf[slot, index].astype(f32)
            cols = pl.ds(pl.multiple_of(half * HALF, HALF), HALF)
            target = outs[index].at[head, :, cols]
            pltpu.make_async_copy(wide.at[slot, index], target, out_sem.at[slot, index]).start()
        return carry

    lax.fori_loop(0, 4, write, 0)
    for slot, (head, half) in enumerate(slots):
        for index in range(3):
            target = outs[index].at[head, :, pl.ds(half * HALF, HALF)]
            done.append(pltpu.make_async_copy(wide.at[slot, index], target, out_sem.at[slot, index]))
    for copy in done:
        copy.wait()


def finish(place, near, opposite, sent):
    return pl.pallas_call(
        final_kernel,
        out_shape=[jax.ShapeDtypeStruct((2, DH, FF), f32)] * 3
        + [jax.ShapeDtypeStruct((GROUPS, 16, 64, DH), f32)],
        in_specs=[SSPEC] + [ANYSPEC] * 9,
        out_specs=[HBMSPEC] * 4,
        scratch_shapes=[
            pltpu.VMEM((4, 3, DH, HALF), bf16),
            pltpu.VMEM((4, 3, DH, HALF), f32),
            pltpu.VMEM((GROUPS, 16, 64, DH), bf16),
            pltpu.VMEM((GROUPS, 16, 64, DH), f32),
            pltpu.SemaphoreType.DMA((4,)),
            pltpu.SemaphoreType.DMA((4, 3)),
            pltpu.SemaphoreType.DMA((GROUPS,)),
            pltpu.SemaphoreType.DMA((GROUPS,)),
        ],
        compiler_params=params(51),
        name="finish",
        cost_estimate=cost(10**6, 15 * MIB),
    )(place, *near, *opposite, *sent)


def ring(far):
    return [(i, (i + far) % 4) for i in range(4)]


SWAP = [(0, 1), (1, 0)]


def swap(value):
    return lax.ppermute(value, "c", SWAP)


def sum_up(partial):
    received = [lax.ppermute(partial[far], "z", ring(far)) for far in (2, 1, 3)]
    total = partial[0].astype(f32)
    for part in received:
        total = total + part.astype(f32)
    return total.astype(bf16)


def gather(value):
    whole = lax.all_gather(value, "z")
    return whole, swap(whole)


def gather_direct(value):
    far2, far1, far3 = [lax.ppermute(value, "z", ring(4 - far)) for far in (2, 1, 3)]
    chunks = [value, far1, far2, far3]
    return chunks + [swap(chunk) for chunk in chunks]


def y_pairs(far, across=0):
    return [(2 * y + (y // 2 ^ across), 2 * ((y + far) % 4) + y // 2) for y in range(4)]


def z_pairs(far):
    cores = [2 * y + ((y + 2) % 4) // 2 for y in range(4)]
    return [(8 * z + core, 8 * ((z + far) % 4) + core) for z in range(4) for core in cores]


def shards(queries, keys, values, rates, step_sizes, w_gate, w_up, w_down):
    z, y, c = lax.axis_index("z"), lax.axis_index("y"), lax.axis_index("c")
    exchange = functools.partial(
        lax.all_to_all, axis_name=("x", "y"), split_axis=0, concat_axis=0, tiled=True
    )
    packed, own = pack(keys, values, rates)
    first = exchange(packed).reshape(TOK, 2 * DH)
    mine = (c == y // 2).astype(jnp.int32)
    stored = (w_gate, w_up, w_down)
    step_local = jnp.broadcast_to(lax.dynamic_index_in_dim(step_sizes, y % 2, 0), (8, LANE))
    place = jnp.stack([c, z, mine, y % 2, y]).astype(jnp.int32)
    others = [swap(w) for w in stored]
    weights, both, step = prepare(place, stored, others, step_local, swap(step_local))
    second = join(own, swap(own), queries, step)
    first = after(first, step, second)
    rest = exchange(after(second, first)).reshape(TOK, 6 * DH)

    chunks = gather(sum_up(grads(place, first, swap(first), both)))
    both, weights, *partial = turn(place, chunks, weights, step, rest)

    early = exchange(forward(rest, both, 4 * DH, partial[0]).reshape(16, 64, DH))
    chunks = gather_direct(sum_up(partial))
    both, quarter, result = close(place, chunks, weights, step, rest, early)
    move = functools.partial(lax.ppermute, axis_name=("y", "c"))
    quarters = [move(quarter, perm=y_pairs(2, across=1))]
    up, down = move(both, perm=y_pairs(1)), move(both, perm=y_pairs(3))
    late = exchange(result.reshape(16, 64, DH))
    for far in (1, 2, 3):
        quarters.append(lax.ppermute(quarters[0], ("z", "y", "c"), z_pairs(4 - far)))
    gate, up, down, outputs = finish(place, [both, up, down], quarters, (early, late))
    return (outputs, gate, up, down)


def solution(mesh):
    grid = Mesh(mesh.devices.reshape(4, 4, 4, 2), ("z", "y", "x", "c"))
    tokens = ("z", "y", "x", "c")
    heads = ("x", "c")
    return jax.shard_map(
        shards,
        mesh=grid,
        in_specs=(
            P(None, None, tokens, None),
            P(None, None, tokens, None),
            P(None, None, tokens, None),
            P(None, None, tokens),
            P(heads),
            P(heads, None, None),
            P(heads, None, None),
            P(heads, None, None),
        ),
        out_specs=(
            P(None, None, tokens, None),
            P(heads, None, None),
            P(heads, None, None),
            P(heads, None, None),
        ),
        check_vma=False,
    )
```

```python
import functools

import jax
import jax.numpy as jnp
from jax import lax
from jax.experimental import pallas as pl
from jax.experimental.pallas import tpu as pltpu
from jax.sharding import Mesh
from jax.sharding import PartitionSpec as P

GROUPS = 2
NS_STEPS = 5
DH = 256
FF = 1024
HALF = FF // 2
LANE = 128
TOK = 1024
TILE = 512

coef_a = 3.4445
coef_b = -4.775
coef_c = 2.0315

f32 = jnp.float32
bf16 = jnp.bfloat16
MIB = 1024 * 1024

VSPEC = pl.BlockSpec(memory_space=pltpu.VMEM)
ANYSPEC = pl.BlockSpec(memory_space=pl.ANY)
HBMSPEC = pl.BlockSpec(memory_space=pltpu.HBM)
SSPEC = pl.BlockSpec(memory_space=pltpu.SMEM)


def dot(a, b, dims):
    return lax.dot_general(a, b, (dims, ((), ())), preferred_element_type=f32)


def params(mib):
    return pltpu.CompilerParams(vmem_limit_bytes=mib * MIB)


def cost(flops, size, transcendentals=0):
    return pl.CostEstimate(flops=flops, bytes_accessed=size, transcendentals=transcendentals)


def after(value, *earlier):
    return lax.optimization_barrier((value, earlier))[0]


def pack_kernel(key_ref, value_ref, rate_ref, *out_refs):
    for group, out_ref in enumerate(out_refs):
        out_ref[:, :, :DH] = key_ref[group]
        rate = -rate_ref[group].astype(f32)
        out_ref[:, :, DH:] = (rate[:, :, None] * value_ref[group].astype(f32)).astype(bf16)


def pack(keys, values, rates):
    heads = 8
    spec = pl.BlockSpec((GROUPS, heads, 64, DH), lambda i: (0, i, 0, 0))
    return pl.pallas_call(
        pack_kernel,
        grid=(16 // heads,),
        out_shape=[jax.ShapeDtypeStruct((16, 64, 2 * DH), bf16)] * GROUPS,
        in_specs=[spec, spec, pl.BlockSpec((GROUPS, heads, 64), lambda i: (0, i, 0))],
        out_specs=[pl.BlockSpec((heads, 64, 2 * DH), lambda i: (i, 0, 0))] * GROUPS,
        compiler_params=params(56),
        name="pack",
        cost_estimate=cost(1, 1),
    )(keys, values, rates)


def join_kernel(own_ref, peer_ref, queries_ref, *refs):
    out_ref = refs[-1]
    out_ref[:, :, : 2 * DH] = own_ref[...]
    out_ref[:, :, 2 * DH : 4 * DH] = peer_ref[...]
    for group in range(GROUPS):
        out_ref[:, :, (4 + group) * DH : (5 + group) * DH] = queries_ref[group]


def join(own, peer, queries, *earlier):
    heads = 8
    spec = pl.BlockSpec((heads, 64, 2 * DH), lambda i: (i, 0, 0))
    return pl.pallas_call(
        join_kernel,
        grid=(16 // heads,),
        out_shape=jax.ShapeDtypeStruct((16, 64, 6 * DH), bf16),
        in_specs=[spec, spec, pl.BlockSpec((2, heads, 64, DH), lambda i: (0, i, 0, 0))]
        + [ANYSPEC] * len(earlier),
        out_specs=pl.BlockSpec((heads, 64, 6 * DH), lambda i: (i, 0, 0)),
        compiler_params=params(56),
        name="join",
        cost_estimate=cost(1, 1),
    )(own, peer, queries, *earlier)


TILES = 2 * TOK // TILE
GRAD_SCRATCH = [
    pltpu.VMEM((3, DH, HALF), f32),
    pltpu.VMEM((TILES, TILE, 2 * DH), bf16),
    pltpu.SemaphoreType.DMA((TILES,)),
]


def token_copies(sides, kd, sem):
    copies = []
    for side, (ref, column) in enumerate(sides):
        for tile in range(TILES // 2):
            source = ref.at[pl.ds(tile * TILE, TILE), pl.ds(column, 2 * DH)]
            at = side * (TILES // 2) + tile
            copies.append(pltpu.make_async_copy(source, kd.at[at], sem.at[at]))
    return copies


def grad_body(kd, kd_sem, wb, acc_ref, out_refs, deep):
    acc_ref[...] = jnp.zeros_like(acc_ref)

    def tile(at, carry):
        pltpu.make_async_copy(kd.at[at], kd.at[at], kd_sem.at[at]).wait()
        key = kd[at, :, :DH]
        dout = kd[at, :, DH:]
        gate = dot(key, wb[0], ((1,), (0,)))
        up = dot(key, wb[1], ((1,), (0,)))
        dhid = dot(dout, wb[2], ((1,), (0,)))
        sigma = 0.5 * jnp.tanh(0.5 * gate) + 0.5
        active = gate * sigma
        hidden = (active * up).astype(bf16)
        d_up = (dhid * active).astype(bf16)
        d_gate = (dhid * up * (sigma + active * (1.0 - sigma))).astype(bf16)
        for index, (left, right) in enumerate(((key, d_gate), (key, d_up), (dout, hidden))):
            acc_ref[index] += dot(left, right, ((0,), (0,)))
        return carry

    lax.fori_loop(0, TILES, tile, 0)
    for far in range(4):
        cols = pl.ds(pl.multiple_of(((deep + far) & 3) * LANE, LANE), LANE)
        out_refs[far][...] = acc_ref[:, :, cols].astype(bf16)


def grad_kernel(place_ref, own_ref, peer_ref, wb_ref, *refs):
    out_refs, (acc_ref, kd, kd_sem, wb, wb_sem) = refs[:4], refs[4:]
    fetch = pltpu.make_async_copy(wb_ref.at[0], wb, wb_sem)
    fetch.start()
    copies = token_copies(((own_ref, 0), (peer_ref, 0)), kd, kd_sem)
    copies[0].start()
    fetch.wait()
    for copy in copies[1:]:
        copy.start()
    grad_body(kd, kd_sem, wb, acc_ref, out_refs, place_ref[1])


def grads(place, own, peer, both):
    return pl.pallas_call(
        grad_kernel,
        out_shape=[jax.ShapeDtypeStruct((3, DH, LANE), bf16)] * 4,
        in_specs=[SSPEC] + [HBMSPEC] * 3,
        out_specs=[VSPEC] * 4,
        scratch_shapes=GRAD_SCRATCH + [pltpu.VMEM((3, DH, HALF), bf16), pltpu.SemaphoreType.DMA(())],
        compiler_params=params(50),
        name="grads",
        cost_estimate=cost(12 * 2 * TOK * DH * HALF, 4 * MIB, 2 * TOK * HALF),
    )(place, own, peer, both)


NS_SCRATCH = [
    pltpu.VMEM((3, DH, FF), bf16),
    pltpu.VMEM((3, 8, DH, LANE), f32),
    pltpu.VMEM((2, 3, DH, HALF), bf16),
    pltpu.SemaphoreType.DMA(()),
]


def renew(weight, value, step):
    cand = weight - step * value.astype(f32)
    scale = jnp.sqrt(jnp.sum(weight * weight, axis=0, keepdims=True) + 1e-06) / jnp.sqrt(
        jnp.sum(cand * cand, axis=0, keepdims=True) + 1e-06
    )
    return cand * scale


def ns_body(grad, w_ref, step_ref, scratch, others, keep):
    ortho, weights, both, sem = scratch
    fetch = pltpu.make_async_copy(w_ref, weights, sem)
    fetch.start()
    for other in others:
        other.start()
    def begin(index, carry):
        total = None
        for half in range(2):
            for chunk in range(4):
                part = grad[half, chunk, index].astype(f32)
                part = part * part
                total = part if total is None else total + part
        total = jnp.sum(jnp.sum(total, axis=0, keepdims=True), axis=1, keepdims=True)
        norm = jnp.sqrt(total) + 1e-07
        for half in range(2):
            for chunk in range(4):
                at = (half * 4 + chunk) * LANE
                unit = (grad[half, chunk, index].astype(f32) / norm).astype(bf16)
                ortho[index, :, at : at + LANE] = unit
        return carry

    def iterate(step, carry):
        grams = [dot(ortho[i], ortho[i], ((1,), (1,))).astype(bf16) for i in range(3)]
        squares = [dot(gram, gram, ((1,), (0,))) for gram in grams]
        polys = [
            (coef_b * gram.astype(f32) + coef_c * square).astype(bf16) for gram, square in zip(grams, squares)
        ]
        for i in range(3):
            moved = dot(polys[i], ortho[i], ((1,), (0,)))
            ortho[i] = (coef_a * ortho[i].astype(f32) + moved).astype(bf16)
        return carry

    def update(index, carry):
        step = step_ref[0:1, 0:1]
        for chunk in range(8):
            value = ortho[index, :, chunk * LANE : (chunk + 1) * LANE]
            fresh = renew(weights[index, chunk], value, step)
            at = (chunk % 4) * LANE
            both[chunk // 4, index, :, at : at + LANE] = fresh.astype(bf16)
            if keep:
                weights[index, chunk] = fresh
        return carry

    lax.fori_loop(0, 3, begin, 0)
    lax.fori_loop(0, NS_STEPS, iterate, 0, unroll=True)
    fetch.wait()
    lax.fori_loop(0, 3, update, 0)


NS_FLOPS = 3 * 1510 * 10**6
BOTH = jax.ShapeDtypeStruct((2, 3, DH, HALF), bf16)


GRAD_PIECES = [pltpu.VMEM((2, 4, 3, DH, LANE), bf16), pltpu.SemaphoreType.DMA((8,))]


def load_pieces(g_refs, grad, sem, deep):
    pieces = []
    for i, ref in enumerate(g_refs):
        if len(g_refs) == 2:
            target = grad.at[i]
        else:
            target = grad.at[i // 4, (deep + i) & 3]
        pieces.append(pltpu.make_async_copy(ref, target, sem.at[i]))
    for piece in pieces:
        piece.start()
    for piece in pieces:
        piece.wait()
    return grad


def turn_kernel(*refs):
    place_ref, g_refs, w_ref, step_ref, rest_ref = refs[0], refs[1:3], *refs[3:6]
    both_ref, wnew_ref, out_refs, scratch = refs[6], refs[7], refs[8:12], refs[12:]
    ns_scratch, (acc_ref, kd, kd_sem), sem = scratch[:4], scratch[4:7], scratch[7]
    weights, both = ns_scratch[1], ns_scratch[2]
    grad = load_pieces(g_refs, *scratch[8:], place_ref[1])
    copies = token_copies(((rest_ref, 0), (rest_ref, 2 * DH)), kd, kd_sem)
    ns_body(grad, w_ref, step_ref, ns_scratch, copies, True)
    done = [
        pltpu.make_async_copy(both, both_ref, sem.at[0]),
        pltpu.make_async_copy(weights, wnew_ref, sem.at[1]),
    ]
    for copy in done:
        copy.start()
    grad_body(kd, kd_sem, both.at[0], acc_ref, out_refs, place_ref[1])
    for copy in done:
        copy.wait()


def turn(place, chunks, weight, step, rest):
    return pl.pallas_call(
        turn_kernel,
        out_shape=[BOTH, jax.ShapeDtypeStruct((3, 8, DH, LANE), f32)]
        + [jax.ShapeDtypeStruct((3, DH, LANE), bf16)] * 4,
        in_specs=[SSPEC] + [ANYSPEC] * 2 + [HBMSPEC, VSPEC, HBMSPEC],
        out_specs=[HBMSPEC] * 2 + [VSPEC] * 4,
        scratch_shapes=NS_SCRATCH + GRAD_SCRATCH + [pltpu.SemaphoreType.DMA((2,))] + GRAD_PIECES,
        compiler_params=params(56),
        name="turn",
        cost_estimate=cost(NS_FLOPS + 12 * 2 * TOK * DH * HALF, 14 * MIB, 2 * TOK * HALF),
    )(place, *chunks, weight, step, rest)


def query_half(queries, weights, half, acc_ref, out_ref, column):
    def tile(at, carry):
        rows = pl.ds(pl.multiple_of(at * TILE, TILE), TILE)
        query = queries[rows, :]
        gate = dot(query, weights[0], ((1,), (0,)))
        up = dot(query, weights[1], ((1,), (0,)))
        hidden = (gate * (0.5 * jnp.tanh(0.5 * gate) + 0.5) * up).astype(bf16)
        part = dot(hidden, weights[2], ((1,), (1,)))
        if half:
            out_ref[rows, column : column + DH] = (acc_ref[rows, :] + part).astype(bf16)
        else:
            acc_ref[rows, :] = part
        return carry

    lax.fori_loop(0, TOK // TILE, tile, 0, unroll=True)


QUERY_SCRATCH = [pltpu.VMEM((TOK, DH), f32), pltpu.VMEM((TOK, DH), bf16), pltpu.SemaphoreType.DMA(())]


def query_kernel(column, rest_ref, both_ref, *refs):
    out_ref, acc_ref, queries, q_sem, both, sem = refs[-6:]
    copies = [pltpu.make_async_copy(both_ref.at[half], both.at[half], sem.at[half]) for half in range(2)]
    fetch = pltpu.make_async_copy(rest_ref.at[:, pl.ds(column, DH)], queries, q_sem)
    fetch.start()
    copies[0].start()
    fetch.wait()
    copies[0].wait()
    copies[1].start()
    query_half(queries, both.at[0], 0, acc_ref, out_ref, 0)
    copies[1].wait()
    query_half(queries, both.at[1], 1, acc_ref, out_ref, 0)


def forward(rest, both, column, *earlier):
    return pl.pallas_call(
        functools.partial(query_kernel, column),
        out_shape=jax.ShapeDtypeStruct((TOK, DH), bf16),
        in_specs=[HBMSPEC] * 2 + [ANYSPEC] * len(earlier),
        out_specs=VSPEC,
        scratch_shapes=QUERY_SCRATCH + [pltpu.VMEM((2, 3, DH, HALF), bf16), pltpu.SemaphoreType.DMA((2,))],
        compiler_params=params(56),
        name="forward",
        cost_estimate=cost(6 * TOK * DH * FF, 3 * MIB, TOK * FF),
    )(rest, both, *earlier)


def close_kernel(*refs):
    place_ref, g_refs, w_ref, step_ref, rest_ref, early_ref = refs[0], refs[1:9], *refs[9:13]
    both_ref, quarter_ref, out_ref, outputs_ref = refs[13:17]
    ns_scratch, pieces, (acc_ref, queries, q_sem), (quarter, sem, narrow, wide) = (
        refs[17:21],
        refs[21:23],
        refs[23:26],
        refs[26:],
    )
    both = ns_scratch[2]
    fetch = pltpu.make_async_copy(rest_ref.at[:, pl.ds(5 * DH, DH)], queries, q_sem)
    early = pltpu.make_async_copy(early_ref, narrow, sem.at[2])
    ns_body(load_pieces(g_refs, *pieces, place_ref[1]), w_ref, step_ref, ns_scratch, [fetch, early], False)
    cols = pl.ds(pl.multiple_of(place_ref[1] * LANE, LANE), LANE)
    for half in range(2):
        quarter[half] = both[half, :, :, cols]
    done = [
        pltpu.make_async_copy(quarter, quarter_ref, sem.at[0]),
        pltpu.make_async_copy(both, both_ref, sem.at[1]),
        pltpu.make_async_copy(wide, outputs_ref.at[0], sem.at[3]),
    ]
    early.wait()
    wide[...] = narrow[...].astype(f32)
    for copy in done:
        copy.start()
    fetch.wait()
    for half in range(2):
        query_half(queries, both.at[half], half, acc_ref, out_ref, 0)
    for copy in done:
        copy.wait()


def close(place, chunks, weight, step, rest, early):
    return pl.pallas_call(
        close_kernel,
        out_shape=[
            BOTH,
            jax.ShapeDtypeStruct((2, 3, DH, LANE), bf16),
            jax.ShapeDtypeStruct((TOK, DH), bf16),
            jax.ShapeDtypeStruct((GROUPS, 16, 64, DH), f32),
        ],
        in_specs=[SSPEC] + [ANYSPEC] * 8 + [HBMSPEC, VSPEC, HBMSPEC, ANYSPEC],
        out_specs=[HBMSPEC, HBMSPEC, VSPEC, HBMSPEC],
        scratch_shapes=NS_SCRATCH
        + GRAD_PIECES
        + QUERY_SCRATCH
        + [
            pltpu.VMEM((2, 3, DH, LANE), bf16),
            pltpu.SemaphoreType.DMA((4,)),
            pltpu.VMEM((16, 64, DH), bf16),
            pltpu.VMEM((16, 64, DH), f32),
        ],
        compiler_params=params(52),
        name="close",
        cost_estimate=cost(NS_FLOPS + 6 * TOK * DH * FF, 10 * MIB, TOK * FF),
    )(place, *chunks, weight, step, rest, early)


def prep_kernel(place_ref, *refs):
    local, other, step_ref, step_other_ref = refs[:3], refs[3:6], refs[6], refs[7]
    wrot_ref, both_ref, step_out_ref, weights, sem, out_sem = refs[8:]
    core, mine, row = place_ref[0], place_ref[2], place_ref[3]
    step_out_ref[...] = jnp.where(mine == 1, step_ref[...], step_other_ref[...])

    def fetch(sources):
        copies = []
        for index in range(3):
            for chunk in range(8):
                block = (core ^ (chunk // 4)) * 4 + chunk % 4
                cols = pl.ds(pl.multiple_of(block * LANE, LANE), LANE)
                copies.append(
                    pltpu.make_async_copy(
                        sources[index].at[row, :, cols], weights.at[index, chunk], sem.at[index, chunk]
                    )
                )
        return copies

    @pl.when(mine == 1)
    def _():
        for copy in fetch(local):
            copy.start()

    @pl.when(mine != 1)
    def _():
        for copy in fetch(other):
            copy.start()

    def cast(index, carry):
        for chunk in range(8):
            pltpu.make_async_copy(weights.at[index, chunk], weights.at[index, chunk], sem.at[index, chunk]).wait()
            at = (chunk % 4) * LANE
            both_ref[chunk // 4, index, :, at : at + LANE] = weights[index, chunk].astype(bf16)
        return carry

    lax.fori_loop(0, 3, cast, 0)
    copy = pltpu.make_async_copy(weights, wrot_ref, out_sem)
    copy.start()
    copy.wait()


def prepare(place, local, other, step, step_other):
    return pl.pallas_call(
        prep_kernel,
        out_shape=(
            jax.ShapeDtypeStruct((3, 8, DH, LANE), f32),
            BOTH,
            jax.ShapeDtypeStruct((8, LANE), f32),
        ),
        in_specs=[SSPEC] + [HBMSPEC] * 6 + [VSPEC] * 2,
        out_specs=(HBMSPEC, VSPEC, VSPEC),
        scratch_shapes=[
            pltpu.VMEM((3, 8, DH, LANE), f32),
            pltpu.SemaphoreType.DMA((3, 8)),
            pltpu.SemaphoreType.DMA(()),
        ],
        compiler_params=params(56),
        name="prepare",
        cost_estimate=cost(1, 1),
    )(place, *local, *other, step, step_other)


def final_kernel(place_ref, *refs):
    near, opposite, late_ref, outs, result_ref = refs[:3], refs[3:7], refs[7], refs[9:12], refs[12]
    buf, wide, late, wide_late, in_sem, out_sem, late_sem, result_sem = refs[13:]
    core, deep, row = place_ref[0], place_ref[1], place_ref[4]
    slots = [(head, half) for head in range(2) for half in range(2)]
    fetch = pltpu.make_async_copy(late_ref, late, late_sem)
    fetch.start()

    def straight(ref, slot, flip):
        pltpu.make_async_copy(ref.at[flip], buf.at[slot], in_sem.at[slot]).start()

    def pieces(slot, flip):
        for far in range(4):
            cols = pl.ds(pl.multiple_of(((deep + far) & 3) * LANE, LANE), LANE)
            source = opposite[far].at[1 - flip]
            pltpu.make_async_copy(source, buf.at[slot, :, :, cols], in_sem.at[slot]).start()

    for slot, (head, half) in enumerate(slots):
        away = (row - 2 * core - head) & 3
        flip = core ^ half
        for at, far in enumerate((0, 1, 3)):
            pl.when(away == far)(functools.partial(straight, near[at], slot, flip))
        pl.when(away == 2)(functools.partial(pieces, slot, flip))
    fetch.wait()
    wide_late[...] = late[...].astype(f32)
    done = [pltpu.make_async_copy(wide_late, result_ref.at[1], result_sem)]
    done[0].start()

    def write(slot, carry):
        head, half = slot // 2, slot % 2
        pltpu.make_async_copy(buf.at[slot], buf.at[slot], in_sem.at[slot]).wait()
        for index in range(3):
            wide[slot, index] = buf[slot, index].astype(f32)
            cols = pl.ds(pl.multiple_of(half * HALF, HALF), HALF)
            target = outs[index].at[head, :, cols]
            pltpu.make_async_copy(wide.at[slot, index], target, out_sem.at[slot, index]).start()
        return carry

    lax.fori_loop(0, 4, write, 0)
    for slot, (head, half) in enumerate(slots):
        for index in range(3):
            target = outs[index].at[head, :, pl.ds(half * HALF, HALF)]
            done.append(pltpu.make_async_copy(wide.at[slot, index], target, out_sem.at[slot, index]))
    for copy in done:
        copy.wait()


def finish(place, near, opposite, late, outputs):
    return pl.pallas_call(
        final_kernel,
        out_shape=[jax.ShapeDtypeStruct((2, DH, FF), f32)] * 3
        + [jax.ShapeDtypeStruct((GROUPS, 16, 64, DH), f32)],
        in_specs=[SSPEC] + [ANYSPEC] * 8 + [HBMSPEC],
        out_specs=[HBMSPEC] * 4,
        scratch_shapes=[
            pltpu.VMEM((4, 3, DH, HALF), bf16),
            pltpu.VMEM((4, 3, DH, HALF), f32),
            pltpu.VMEM((16, 64, DH), bf16),
            pltpu.VMEM((16, 64, DH), f32),
            pltpu.SemaphoreType.DMA((4,)),
            pltpu.SemaphoreType.DMA((4, 3)),
            pltpu.SemaphoreType.DMA(()),
            pltpu.SemaphoreType.DMA(()),
        ],
        input_output_aliases={9: 3},
        compiler_params=params(51),
        name="finish",
        cost_estimate=cost(10**6, 15 * MIB),
    )(place, *near, *opposite, late, outputs)


def ring(far):
    return [(i, (i + far) % 4) for i in range(4)]


SWAP = [(0, 1), (1, 0)]


def swap(value):
    return lax.ppermute(value, "c", SWAP)


def sum_up(partial):
    received = [lax.ppermute(partial[far], "z", ring(far)) for far in (2, 1, 3)]
    total = partial[0].astype(f32)
    for part in received:
        total = total + part.astype(f32)
    return total.astype(bf16)


def gather(value):
    whole = lax.all_gather(value, "z")
    return whole, swap(whole)


def gather_direct(value):
    far2, far1, far3 = [lax.ppermute(value, "z", ring(4 - far)) for far in (2, 1, 3)]
    chunks = [value, far1, far2, far3]
    return chunks + [swap(chunk) for chunk in chunks]


def y_pairs(far, across=0):
    return [(2 * y + (y // 2 ^ across), 2 * ((y + far) % 4) + y // 2) for y in range(4)]


def z_pairs(far):
    cores = [2 * y + ((y + 2) % 4) // 2 for y in range(4)]
    return [(8 * z + core, 8 * ((z + far) % 4) + core) for z in range(4) for core in cores]


def shards(queries, keys, values, rates, step_sizes, w_gate, w_up, w_down):
    z, y, c = lax.axis_index("z"), lax.axis_index("y"), lax.axis_index("c")
    exchange = functools.partial(
        lax.all_to_all, axis_name=("x", "y"), split_axis=0, concat_axis=0, tiled=True
    )
    packed, own = pack(keys, values, rates)
    first = exchange(packed).reshape(TOK, 2 * DH)
    mine = (c == y // 2).astype(jnp.int32)
    stored = (w_gate, w_up, w_down)
    step_local = jnp.broadcast_to(lax.dynamic_index_in_dim(step_sizes, y % 2, 0), (8, LANE))
    place = jnp.stack([c, z, mine, y % 2, y]).astype(jnp.int32)
    others = [swap(w) for w in stored]
    weights, both, step = prepare(place, stored, others, step_local, swap(step_local))
    second = join(own, swap(own), queries, step)
    first = after(first, step, second)
    rest = exchange(after(second, first)).reshape(TOK, 6 * DH)

    chunks = gather(sum_up(grads(place, first, swap(first), both)))
    both, weights, *partial = turn(place, chunks, weights, step, rest)

    early = exchange(forward(rest, both, 4 * DH, partial[0]).reshape(16, 64, DH))
    chunks = gather_direct(sum_up(partial))
    both, quarter, result, outputs = close(place, chunks, weights, step, rest, early)
    move = functools.partial(lax.ppermute, axis_name=("y", "c"))
    quarters = [move(quarter, perm=y_pairs(2, across=1))]
    up, down = move(both, perm=y_pairs(1)), move(both, perm=y_pairs(3))
    late = exchange(result.reshape(16, 64, DH))
    for far in (1, 2, 3):
        quarters.append(lax.ppermute(quarters[0], ("z", "y", "c"), z_pairs(4 - far)))
    gate, up, down, outputs = finish(place, [both, up, down], quarters, late, outputs)
    return (outputs, gate, up, down)


def solution(mesh):
    grid = Mesh(mesh.devices.reshape(4, 4, 4, 2), ("z", "y", "x", "c"))
    tokens = ("z", "y", "x", "c")
    heads = ("x", "c")
    return jax.shard_map(
        shards,
        mesh=grid,
        in_specs=(
            P(None, None, tokens, None),
            P(None, None, tokens, None),
            P(None, None, tokens, None),
            P(None, None, tokens),
            P(heads),
            P(heads, None, None),
            P(heads, None, None),
            P(heads, None, None),
        ),
        out_specs=(
            P(None, None, tokens, None),
            P(heads, None, None),
            P(heads, None, None),
            P(heads, None, None),
        ),
        check_vma=False,
    )
```

```python
import functools

import jax
import jax.numpy as jnp
from jax import lax
from jax.experimental import pallas as pl
from jax.experimental.pallas import tpu as pltpu
from jax.sharding import Mesh
from jax.sharding import PartitionSpec as P

GROUPS = 2
NS_STEPS = 5
DH = 256
FF = 1024
HALF = FF // 2
LANE = 128
TOK = 1024
TILE = 512

coef_a = 3.4445
coef_b = -4.775
coef_c = 2.0315

f32 = jnp.float32
bf16 = jnp.bfloat16
MIB = 1024 * 1024

VSPEC = pl.BlockSpec(memory_space=pltpu.VMEM)
ANYSPEC = pl.BlockSpec(memory_space=pl.ANY)
HBMSPEC = pl.BlockSpec(memory_space=pltpu.HBM)
SSPEC = pl.BlockSpec(memory_space=pltpu.SMEM)


def dot(a, b, dims):
    return lax.dot_general(a, b, (dims, ((), ())), preferred_element_type=f32)


def params(mib):
    return pltpu.CompilerParams(vmem_limit_bytes=mib * MIB)


def cost(flops, size, transcendentals=0):
    return pl.CostEstimate(flops=flops, bytes_accessed=size, transcendentals=transcendentals)


def after(value, *earlier):
    return lax.optimization_barrier((value, earlier))[0]


def pack_kernel(key_ref, value_ref, rate_ref, *out_refs):
    for group, out_ref in enumerate(out_refs):
        out_ref[:, :, :DH] = key_ref[group]
        rate = -rate_ref[group].astype(f32)
        out_ref[:, :, DH:] = (rate[:, :, None] * value_ref[group].astype(f32)).astype(bf16)


def pack(keys, values, rates):
    heads = 8
    spec = pl.BlockSpec((GROUPS, heads, 64, DH), lambda i: (0, i, 0, 0))
    return pl.pallas_call(
        pack_kernel,
        grid=(16 // heads,),
        out_shape=[jax.ShapeDtypeStruct((16, 64, 2 * DH), bf16)] * GROUPS,
        in_specs=[spec, spec, pl.BlockSpec((GROUPS, heads, 64), lambda i: (0, i, 0))],
        out_specs=[pl.BlockSpec((heads, 64, 2 * DH), lambda i: (i, 0, 0))] * GROUPS,
        compiler_params=params(56),
        name="pack",
        cost_estimate=cost(1, 1),
    )(keys, values, rates)


def join_kernel(own_ref, peer_ref, queries_ref, *refs):
    out_ref = refs[-1]
    out_ref[:, :, : 2 * DH] = own_ref[...]
    out_ref[:, :, 2 * DH : 4 * DH] = peer_ref[...]
    for group in range(GROUPS):
        out_ref[:, :, (4 + group) * DH : (5 + group) * DH] = queries_ref[group]


def join(own, peer, queries, *earlier):
    heads = 8
    spec = pl.BlockSpec((heads, 64, 2 * DH), lambda i: (i, 0, 0))
    return pl.pallas_call(
        join_kernel,
        grid=(16 // heads,),
        out_shape=jax.ShapeDtypeStruct((16, 64, 6 * DH), bf16),
        in_specs=[spec, spec, pl.BlockSpec((2, heads, 64, DH), lambda i: (0, i, 0, 0))]
        + [ANYSPEC] * len(earlier),
        out_specs=pl.BlockSpec((heads, 64, 6 * DH), lambda i: (i, 0, 0)),
        compiler_params=params(56),
        name="join",
        cost_estimate=cost(1, 1),
    )(own, peer, queries, *earlier)


TILES = 2 * TOK // TILE
GRAD_SCRATCH = [
    pltpu.VMEM((3, DH, HALF), f32),
    pltpu.VMEM((TILES, TILE, 2 * DH), bf16),
    pltpu.SemaphoreType.DMA((TILES,)),
]


def token_copies(sides, kd, sem):
    copies = []
    for side, (ref, column) in enumerate(sides):
        for tile in range(TILES // 2):
            source = ref.at[pl.ds(tile * TILE, TILE), pl.ds(column, 2 * DH)]
            at = side * (TILES // 2) + tile
            copies.append(pltpu.make_async_copy(source, kd.at[at], sem.at[at]))
    return copies


def grad_body(kd, kd_sem, wb, acc_ref, out_refs, deep):
    acc_ref[...] = jnp.zeros_like(acc_ref)

    def tile(at, carry):
        pltpu.make_async_copy(kd.at[at], kd.at[at], kd_sem.at[at]).wait()
        key = kd[at, :, :DH]
        dout = kd[at, :, DH:]
        gate = dot(key, wb[0], ((1,), (0,)))
        up = dot(key, wb[1], ((1,), (0,)))
        dhid = dot(dout, wb[2], ((1,), (0,)))
        sigma = 0.5 * jnp.tanh(0.5 * gate) + 0.5
        active = gate * sigma
        hidden = (active * up).astype(bf16)
        d_up = (dhid * active).astype(bf16)
        d_gate = (dhid * up * (sigma + active * (1.0 - sigma))).astype(bf16)
        for index, (left, right) in enumerate(((key, d_gate), (key, d_up), (dout, hidden))):
            acc_ref[index] += dot(left, right, ((0,), (0,)))
        return carry

    lax.fori_loop(0, TILES, tile, 0)
    for far in range(4):
        cols = pl.ds(pl.multiple_of(((deep + far) & 3) * LANE, LANE), LANE)
        out_refs[far][...] = acc_ref[:, :, cols].astype(bf16)


def grad_kernel(place_ref, own_ref, peer_ref, wb_ref, *refs):
    out_refs, (acc_ref, kd, kd_sem, wb, wb_sem) = refs[:4], refs[4:]
    fetch = pltpu.make_async_copy(wb_ref.at[0], wb, wb_sem)
    fetch.start()
    copies = token_copies(((own_ref, 0), (peer_ref, 0)), kd, kd_sem)
    copies[0].start()
    fetch.wait()
    for copy in copies[1:]:
        copy.start()
    grad_body(kd, kd_sem, wb, acc_ref, out_refs, place_ref[1])


def grads(place, own, peer, both):
    return pl.pallas_call(
        grad_kernel,
        out_shape=[jax.ShapeDtypeStruct((3, DH, LANE), bf16)] * 4,
        in_specs=[SSPEC] + [HBMSPEC] * 3,
        out_specs=[VSPEC] * 4,
        scratch_shapes=GRAD_SCRATCH + [pltpu.VMEM((3, DH, HALF), bf16), pltpu.SemaphoreType.DMA(())],
        compiler_params=params(50),
        name="grads",
        cost_estimate=cost(12 * 2 * TOK * DH * HALF, 4 * MIB, 2 * TOK * HALF),
    )(place, own, peer, both)


NS_SCRATCH = [
    pltpu.VMEM((3, DH, FF), bf16),
    pltpu.VMEM((3, 8, DH, LANE), f32),
    pltpu.VMEM((2, 3, DH, HALF), bf16),
    pltpu.SemaphoreType.DMA(()),
]


def renew(weight, value, step):
    cand = weight - step * value.astype(f32)
    scale = jnp.sqrt(jnp.sum(weight * weight, axis=0, keepdims=True) + 1e-06) / jnp.sqrt(
        jnp.sum(cand * cand, axis=0, keepdims=True) + 1e-06
    )
    return cand * scale


def ns_body(grad, w_ref, step_ref, scratch, others, keep):
    ortho, weights, both, sem = scratch
    fetch = pltpu.make_async_copy(w_ref, weights, sem)
    fetch.start()
    for other in others:
        other.start()
    def begin(index, carry):
        total = None
        for half in range(2):
            for chunk in range(4):
                part = grad[half, chunk, index].astype(f32)
                part = part * part
                total = part if total is None else total + part
        total = jnp.sum(jnp.sum(total, axis=0, keepdims=True), axis=1, keepdims=True)
        norm = jnp.sqrt(total) + 1e-07
        for half in range(2):
            for chunk in range(4):
                at = (half * 4 + chunk) * LANE
                unit = (grad[half, chunk, index].astype(f32) / norm).astype(bf16)
                ortho[index, :, at : at + LANE] = unit
        return carry

    def iterate(step, carry):
        grams = [dot(ortho[i], ortho[i], ((1,), (1,))).astype(bf16) for i in range(3)]
        squares = [dot(gram, gram, ((1,), (0,))) for gram in grams]
        polys = [
            (coef_b * gram.astype(f32) + coef_c * square).astype(bf16) for gram, square in zip(grams, squares)
        ]
        for i in range(3):
            moved = dot(polys[i], ortho[i], ((1,), (0,)))
            ortho[i] = (coef_a * ortho[i].astype(f32) + moved).astype(bf16)
        return carry

    def update(index, carry):
        step = step_ref[0:1, 0:1]
        for chunk in range(8):
            value = ortho[index, :, chunk * LANE : (chunk + 1) * LANE]
            fresh = renew(weights[index, chunk], value, step)
            at = (chunk % 4) * LANE
            both[chunk // 4, index, :, at : at + LANE] = fresh.astype(bf16)
            if keep:
                weights[index, chunk] = fresh
        return carry

    lax.fori_loop(0, 3, begin, 0)
    lax.fori_loop(0, NS_STEPS, iterate, 0, unroll=True)
    fetch.wait()
    lax.fori_loop(0, 3, update, 0)


NS_FLOPS = 3 * 1510 * 10**6
BOTH = jax.ShapeDtypeStruct((2, 3, DH, HALF), bf16)


GRAD_PIECES = [pltpu.VMEM((2, 4, 3, DH, LANE), bf16), pltpu.SemaphoreType.DMA((8,))]


def load_pieces(g_refs, grad, sem, deep):
    pieces = []
    for i, ref in enumerate(g_refs):
        if len(g_refs) == 2:
            target = grad.at[i]
        else:
            target = grad.at[i // 4, (deep + i) & 3]
        pieces.append(pltpu.make_async_copy(ref, target, sem.at[i]))
    for piece in pieces:
        piece.start()
    for piece in pieces:
        piece.wait()
    return grad


def turn_kernel(*refs):
    place_ref, g_refs, w_ref, step_ref, rest_ref = refs[0], refs[1:3], *refs[3:6]
    both_ref, wnew_ref, out_refs, scratch = refs[6], refs[7], refs[8:12], refs[12:]
    ns_scratch, (acc_ref, kd, kd_sem), sem = scratch[:4], scratch[4:7], scratch[7]
    weights, both = ns_scratch[1], ns_scratch[2]
    grad = load_pieces(g_refs, *scratch[8:], place_ref[1])
    copies = token_copies(((rest_ref, 0), (rest_ref, 2 * DH)), kd, kd_sem)
    ns_body(grad, w_ref, step_ref, ns_scratch, copies, True)
    done = [
        pltpu.make_async_copy(both, both_ref, sem.at[0]),
        pltpu.make_async_copy(weights, wnew_ref, sem.at[1]),
    ]
    for copy in done:
        copy.start()
    grad_body(kd, kd_sem, both.at[0], acc_ref, out_refs, place_ref[1])
    for copy in done:
        copy.wait()


def turn(place, chunks, weight, step, rest):
    return pl.pallas_call(
        turn_kernel,
        out_shape=[BOTH, jax.ShapeDtypeStruct((3, 8, DH, LANE), f32)]
        + [jax.ShapeDtypeStruct((3, DH, LANE), bf16)] * 4,
        in_specs=[SSPEC] + [ANYSPEC] * 2 + [HBMSPEC, VSPEC, HBMSPEC],
        out_specs=[HBMSPEC] * 2 + [VSPEC] * 4,
        scratch_shapes=NS_SCRATCH + GRAD_SCRATCH + [pltpu.SemaphoreType.DMA((2,))] + GRAD_PIECES,
        compiler_params=params(50),
        name="turn",
        cost_estimate=cost(NS_FLOPS + 12 * 2 * TOK * DH * HALF, 14 * MIB, 2 * TOK * HALF),
    )(place, *chunks, weight, step, rest)


def query_half(queries, weights, half, acc_ref, out_ref, column):
    def tile(at, carry):
        rows = pl.ds(pl.multiple_of(at * TILE, TILE), TILE)
        query = queries[rows, :]
        gate = dot(query, weights[0], ((1,), (0,)))
        up = dot(query, weights[1], ((1,), (0,)))
        hidden = (gate * (0.5 * jnp.tanh(0.5 * gate) + 0.5) * up).astype(bf16)
        part = dot(hidden, weights[2], ((1,), (1,)))
        if half:
            out_ref[rows, column : column + DH] = (acc_ref[rows, :] + part).astype(bf16)
        else:
            acc_ref[rows, :] = part
        return carry

    lax.fori_loop(0, TOK // TILE, tile, 0, unroll=True)


QUERY_SCRATCH = [pltpu.VMEM((TOK, DH), f32), pltpu.VMEM((TOK, DH), bf16), pltpu.SemaphoreType.DMA(())]


def query_kernel(column, rest_ref, both_ref, *refs):
    out_ref, acc_ref, queries, q_sem, both, sem = refs[-6:]
    copies = [pltpu.make_async_copy(both_ref.at[half], both.at[half], sem.at[half]) for half in range(2)]
    fetch = pltpu.make_async_copy(rest_ref.at[:, pl.ds(column, DH)], queries, q_sem)
    fetch.start()
    copies[0].start()
    fetch.wait()
    copies[0].wait()
    copies[1].start()
    query_half(queries, both.at[0], 0, acc_ref, out_ref, 0)
    copies[1].wait()
    query_half(queries, both.at[1], 1, acc_ref, out_ref, 0)


def forward(rest, both, column, *earlier):
    return pl.pallas_call(
        functools.partial(query_kernel, column),
        out_shape=jax.ShapeDtypeStruct((TOK, DH), bf16),
        in_specs=[HBMSPEC] * 2 + [ANYSPEC] * len(earlier),
        out_specs=VSPEC,
        scratch_shapes=QUERY_SCRATCH + [pltpu.VMEM((2, 3, DH, HALF), bf16), pltpu.SemaphoreType.DMA((2,))],
        compiler_params=params(56),
        name="forward",
        cost_estimate=cost(6 * TOK * DH * FF, 3 * MIB, TOK * FF),
    )(rest, both, *earlier)


def close_kernel(*refs):
    place_ref, g_refs, w_ref, step_ref, rest_ref, early_ref = refs[0], refs[1:9], *refs[9:13]
    both_ref, quarter_ref, out_ref, outputs_ref = refs[13:17]
    ns_scratch, pieces, (acc_ref, queries, q_sem), (quarter, sem, narrow, wide) = (
        refs[17:21],
        refs[21:23],
        refs[23:26],
        refs[26:],
    )
    both = ns_scratch[2]
    fetch = pltpu.make_async_copy(rest_ref.at[:, pl.ds(5 * DH, DH)], queries, q_sem)
    early = pltpu.make_async_copy(early_ref, narrow, sem.at[2])
    ns_body(load_pieces(g_refs, *pieces, place_ref[1]), w_ref, step_ref, ns_scratch, [fetch, early], False)
    cols = pl.ds(pl.multiple_of(place_ref[1] * LANE, LANE), LANE)
    for half in range(2):
        quarter[half] = both[half, :, :, cols]
    done = [
        pltpu.make_async_copy(quarter, quarter_ref, sem.at[0]),
        pltpu.make_async_copy(both, both_ref, sem.at[1]),
        pltpu.make_async_copy(wide, outputs_ref.at[0], sem.at[3]),
    ]
    early.wait()
    wide[...] = narrow[...].astype(f32)
    for copy in done:
        copy.start()
    fetch.wait()
    for half in range(2):
        query_half(queries, both.at[half], half, acc_ref, out_ref, 0)
    for copy in done:
        copy.wait()


def close(place, chunks, weight, step, rest, early):
    return pl.pallas_call(
        close_kernel,
        out_shape=[
            BOTH,
            jax.ShapeDtypeStruct((2, 3, DH, LANE), bf16),
            jax.ShapeDtypeStruct((TOK, DH), bf16),
            jax.ShapeDtypeStruct((GROUPS, 16, 64, DH), f32),
        ],
        in_specs=[SSPEC] + [ANYSPEC] * 8 + [HBMSPEC, VSPEC, HBMSPEC, ANYSPEC],
        out_specs=[HBMSPEC, HBMSPEC, VSPEC, HBMSPEC],
        scratch_shapes=NS_SCRATCH
        + GRAD_PIECES
        + QUERY_SCRATCH
        + [
            pltpu.VMEM((2, 3, DH, LANE), bf16),
            pltpu.SemaphoreType.DMA((4,)),
            pltpu.VMEM((16, 64, DH), bf16),
            pltpu.VMEM((16, 64, DH), f32),
        ],
        compiler_params=params(52),
        name="close",
        cost_estimate=cost(NS_FLOPS + 6 * TOK * DH * FF, 10 * MIB, TOK * FF),
    )(place, *chunks, weight, step, rest, early)


def prep_kernel(place_ref, *refs):
    local, other, step_ref, step_other_ref = refs[:3], refs[3:6], refs[6], refs[7]
    wrot_ref, both_ref, step_out_ref, weights, sem, out_sem = refs[8:]
    core, mine, row = place_ref[0], place_ref[2], place_ref[3]
    step_out_ref[...] = jnp.where(mine == 1, step_ref[...], step_other_ref[...])

    def fetch(sources):
        copies = []
        for index in range(3):
            for chunk in range(8):
                block = (core ^ (chunk // 4)) * 4 + chunk % 4
                cols = pl.ds(pl.multiple_of(block * LANE, LANE), LANE)
                copies.append(
                    pltpu.make_async_copy(
                        sources[index].at[row, :, cols], weights.at[index, chunk], sem.at[index, chunk]
                    )
                )
        return copies

    @pl.when(mine == 1)
    def _():
        for copy in fetch(local):
            copy.start()

    @pl.when(mine != 1)
    def _():
        for copy in fetch(other):
            copy.start()

    def cast(index, carry):
        for chunk in range(8):
            pltpu.make_async_copy(weights.at[index, chunk], weights.at[index, chunk], sem.at[index, chunk]).wait()
            at = (chunk % 4) * LANE
            both_ref[chunk // 4, index, :, at : at + LANE] = weights[index, chunk].astype(bf16)
        return carry

    lax.fori_loop(0, 3, cast, 0)
    copy = pltpu.make_async_copy(weights, wrot_ref, out_sem)
    copy.start()
    copy.wait()


def prepare(place, local, other, step, step_other):
    return pl.pallas_call(
        prep_kernel,
        out_shape=(
            jax.ShapeDtypeStruct((3, 8, DH, LANE), f32),
            BOTH,
            jax.ShapeDtypeStruct((8, LANE), f32),
        ),
        in_specs=[SSPEC] + [HBMSPEC] * 6 + [VSPEC] * 2,
        out_specs=(HBMSPEC, VSPEC, VSPEC),
        scratch_shapes=[
            pltpu.VMEM((3, 8, DH, LANE), f32),
            pltpu.SemaphoreType.DMA((3, 8)),
            pltpu.SemaphoreType.DMA(()),
        ],
        compiler_params=params(56),
        name="prepare",
        cost_estimate=cost(1, 1),
    )(place, *local, *other, step, step_other)


def final_kernel(place_ref, *refs):
    near, opposite, late_ref, outs, result_ref = refs[:3], refs[3:7], refs[7], refs[9:12], refs[12]
    buf, wide, late, wide_late, in_sem, out_sem, late_sem, result_sem = refs[13:]
    core, deep, row = place_ref[0], place_ref[1], place_ref[4]
    slots = [(head, half) for head in range(2) for half in range(2)]
    fetch = pltpu.make_async_copy(late_ref, late, late_sem)
    fetch.start()

    def straight(ref, slot, flip):
        pltpu.make_async_copy(ref.at[flip], buf.at[slot], in_sem.at[slot]).start()

    def pieces(slot, flip):
        for far in range(4):
            cols = pl.ds(pl.multiple_of(((deep + far) & 3) * LANE, LANE), LANE)
            source = opposite[far].at[1 - flip]
            pltpu.make_async_copy(source, buf.at[slot, :, :, cols], in_sem.at[slot]).start()

    for slot, (head, half) in enumerate(slots):
        away = (row - 2 * core - head) & 3
        flip = core ^ half
        for at, far in enumerate((0, 1, 3)):
            pl.when(away == far)(functools.partial(straight, near[at], slot, flip))
        pl.when(away == 2)(functools.partial(pieces, slot, flip))
    fetch.wait()
    wide_late[...] = late[...].astype(f32)
    done = [pltpu.make_async_copy(wide_late, result_ref.at[1], result_sem)]
    done[0].start()

    def write(slot, carry):
        head, half = slot // 2, slot % 2
        pltpu.make_async_copy(buf.at[slot], buf.at[slot], in_sem.at[slot]).wait()
        for index in range(3):
            wide[slot, index] = buf[slot, index].astype(f32)
            cols = pl.ds(pl.multiple_of(half * HALF, HALF), HALF)
            target = outs[index].at[head, :, cols]
            pltpu.make_async_copy(wide.at[slot, index], target, out_sem.at[slot, index]).start()
        return carry

    lax.fori_loop(0, 4, write, 0)
    for slot, (head, half) in enumerate(slots):
        for index in range(3):
            target = outs[index].at[head, :, pl.ds(half * HALF, HALF)]
            done.append(pltpu.make_async_copy(wide.at[slot, index], target, out_sem.at[slot, index]))
    for copy in done:
        copy.wait()


def finish(place, near, opposite, late, outputs):
    return pl.pallas_call(
        final_kernel,
        out_shape=[jax.ShapeDtypeStruct((2, DH, FF), f32)] * 3
        + [jax.ShapeDtypeStruct((GROUPS, 16, 64, DH), f32)],
        in_specs=[SSPEC] + [ANYSPEC] * 8 + [HBMSPEC],
        out_specs=[HBMSPEC] * 4,
        scratch_shapes=[
            pltpu.VMEM((4, 3, DH, HALF), bf16),
            pltpu.VMEM((4, 3, DH, HALF), f32),
            pltpu.VMEM((16, 64, DH), bf16),
            pltpu.VMEM((16, 64, DH), f32),
            pltpu.SemaphoreType.DMA((4,)),
            pltpu.SemaphoreType.DMA((4, 3)),
            pltpu.SemaphoreType.DMA(()),
            pltpu.SemaphoreType.DMA(()),
        ],
        input_output_aliases={9: 3},
        compiler_params=params(51),
        name="finish",
        cost_estimate=cost(10**6, 15 * MIB),
    )(place, *near, *opposite, late, outputs)


def ring(far):
    return [(i, (i + far) % 4) for i in range(4)]


SWAP = [(0, 1), (1, 0)]


def swap(value):
    return lax.ppermute(value, "c", SWAP)


def sum_up(partial):
    received = [lax.ppermute(partial[far], "z", ring(far)) for far in (2, 1, 3)]
    total = partial[0].astype(f32)
    for part in received:
        total = total + part.astype(f32)
    return total.astype(bf16)


def gather(value):
    whole = lax.all_gather(value, "z")
    return whole, swap(whole)


def gather_direct(value):
    far2, far1, far3 = [lax.ppermute(value, "z", ring(4 - far)) for far in (2, 1, 3)]
    chunks = [value, far1, far2, far3]
    return chunks + [swap(chunk) for chunk in chunks]


def y_pairs(far, across=0):
    return [(2 * y + (y // 2 ^ across), 2 * ((y + far) % 4) + y // 2) for y in range(4)]


def z_pairs(far):
    cores = [2 * y + ((y + 2) % 4) // 2 for y in range(4)]
    return [(8 * z + core, 8 * ((z + far) % 4) + core) for z in range(4) for core in cores]


def shards(queries, keys, values, rates, step_sizes, w_gate, w_up, w_down):
    z, y, c = lax.axis_index("z"), lax.axis_index("y"), lax.axis_index("c")
    exchange = functools.partial(
        lax.all_to_all, axis_name=("x", "y"), split_axis=0, concat_axis=0, tiled=True
    )
    packed, own = pack(keys, values, rates)
    first = exchange(packed).reshape(TOK, 2 * DH)
    mine = (c == y // 2).astype(jnp.int32)
    stored = (w_gate, w_up, w_down)
    step_local = jnp.broadcast_to(lax.dynamic_index_in_dim(step_sizes, y % 2, 0), (8, LANE))
    place = jnp.stack([c, z, mine, y % 2, y]).astype(jnp.int32)
    others = [swap(w) for w in stored]
    weights, both, step = prepare(place, stored, others, step_local, swap(step_local))
    second = join(own, swap(own), queries, step)
    first = after(first, step, second)
    rest = exchange(after(second, first)).reshape(TOK, 6 * DH)

    chunks = gather(sum_up(grads(place, first, swap(first), both)))
    both, weights, *partial = turn(place, chunks, weights, step, rest)

    early = exchange(forward(rest, both, 4 * DH, partial[0]).reshape(16, 64, DH))
    chunks = gather_direct(sum_up(partial))
    both, quarter, result, outputs = close(place, chunks, weights, step, rest, early)
    move = functools.partial(lax.ppermute, axis_name=("y", "c"))
    quarters = [move(quarter, perm=y_pairs(2, across=1))]
    up, down = move(both, perm=y_pairs(1)), move(both, perm=y_pairs(3))
    late = exchange(result.reshape(16, 64, DH))
    for far in (1, 2, 3):
        quarters.append(lax.ppermute(quarters[0], ("z", "y", "c"), z_pairs(4 - far)))
    gate, up, down, outputs = finish(place, [both, up, down], quarters, late, outputs)
    return (outputs, gate, up, down)


def solution(mesh):
    grid = Mesh(mesh.devices.reshape(4, 4, 4, 2), ("z", "y", "x", "c"))
    tokens = ("z", "y", "x", "c")
    heads = ("x", "c")
    return jax.shard_map(
        shards,
        mesh=grid,
        in_specs=(
            P(None, None, tokens, None),
            P(None, None, tokens, None),
            P(None, None, tokens, None),
            P(None, None, tokens),
            P(heads),
            P(heads, None, None),
            P(heads, None, None),
            P(heads, None, None),
        ),
        out_specs=(
            P(None, None, tokens, None),
            P(heads, None, None),
            P(heads, None, None),
            P(heads, None, None),
        ),
        check_vma=False,
    )
```
